128 devices in a mesh: ctx: 16 (over x_lo, z, core), tp: 8 (over y, x_hi).
Axes of the slice: x: 4 (x_hi: 2, x_lo: 2; x = x_hi * 2 + x_lo), y: 4, z: 4, core: 2. Of those that a mesh axis runs over, the one named last changes fastest.
Arguments:
- tokens: bfloat16 [16384, 1024], P(('ctx', 'tp')), may hold values from -6 to 6
- block_table: int32 [16, 2], replicated, may hold values from 0 to 31, as said below
- doc_ids: int32 [4, 4096], replicated, may hold values from 0 to 3, never falling along the last dimension, each value on 1 to 2048 neighbouring positions
- attn_gain: bfloat16 [1024], P('ctx'), may hold values from 0.25 to 1.75
- w_query: bfloat16 [1024, 2048], P('ctx', 'tp'), may hold values from -0.1875 to 0.1875
- w_key: bfloat16 [1024, 1024], P('ctx', 'tp'), may hold values from -0.1875 to 0.1875
- w_value: bfloat16 [1024, 1024], P('ctx', 'tp'), may hold values from -0.1875 to 0.1875
- query_gain: bfloat16 [128], P('ctx'), may hold values from 0.25 to 1.75
- key_gain: bfloat16 [128], P('ctx'), may hold values from 0.25 to 1.75
- w_out: bfloat16 [2048, 1024], P('tp', 'ctx'), may hold values from -1 to 1
- ffn_gain: bfloat16 [1024], P('ctx'), may hold values from 0.25 to 1.75
- w_gate: bfloat16 [1024, 3072], P('ctx', 'tp'), may hold values from -0.1875 to 0.1875
- w_up: bfloat16 [1024, 3072], P('ctx', 'tp'), may hold values from -0.1875 to 0.1875
- w_down: bfloat16 [3072, 1024], P('tp', 'ctx'), may hold values from -0.109375 to 0.109375
- out_grad: bfloat16 [16384, 1024], P(('ctx', 'tp')), may hold values from -6 to 6
Outputs:
- out: bfloat16 [16384, 1024], P(('ctx', 'tp'))
- grad_x: bfloat16 [16384, 1024], P(('ctx', 'tp'))
- grad_attn_gain: float32 [1024], P('ctx')
- grad_w_query: float32 [1024, 2048], P('ctx', 'tp')
- grad_w_key: float32 [1024, 1024], P('ctx', 'tp')
- grad_w_value: float32 [1024, 1024], P('ctx', 'tp')
- grad_query_gain: float32 [128], P('ctx')
- grad_key_gain: float32 [128], P('ctx')
- grad_w_out: float32 [2048, 1024], P('tp', 'ctx')
- grad_ffn_gain: float32 [1024], P('ctx')
- grad_w_gate: float32 [1024, 3072], P('ctx', 'tp')
- grad_w_up: float32 [1024, 3072], P('ctx', 'tp')
- grad_w_down: float32 [3072, 1024], P('tp', 'ctx')
The draws below stay inside these ranges and needn't reach their ends.
Inputs may be any that keep to these rules, and one draw needn't show every extreme that they name: `block_table`: row c holds a block b below 16 and its mirror 2 * 16 - 1 - b; the first entries of the rows form a permutation, so every block appears once. `doc_ids`: never falling along a row; each document has 1 to 2048 positions, one exactly that many.
All inputs are finite; a program needn't handle non-finite values.
Results may differ from the reference program's by a relative error of at most 0.025.
Values may be sent and summed in bfloat16 or wider, within the bound.
No kernel may reach another device: no remote copies, remote signals or barrier semaphores. Data moves between devices by JAX's collectives and lax.ppermute only.
A program may use at most 192 MiB of HBM per device.

```python
import math
import jax
import jax.numpy as jnp
import numpy as np
from jax import lax

D = 1024
H = 16
KV = 8
HD = 128
FF = 3072
SEQS = 4
BLK = 128
PAIRS = 16
LENGTH = 4096
LOCAL = 1024
TOKENS = 16384


def draw_block_table(key, part):
    ordering = jax.random.permutation(key, PAIRS).astype(jnp.int32)
    return jnp.stack([ordering, 2 * PAIRS - 1 - ordering], axis=1).astype(jnp.int32)


def level_of(own_key, dims, pieces, least, top_value):
    def one(axis_at, shards_of):
        steps = jax.random.uniform(jax.random.fold_in(jax.random.fold_in(own_key, 6), axis_at), (shards_of,), jnp.float32, least / len(pieces), top_value / len(pieces))
        return jnp.repeat(jnp.exp(steps), dims[axis_at] // shards_of).reshape((-1,) + (1,) * (len(dims) - axis_at - 1))

    gain = one(*pieces[0])
    for cut in pieces[1:]:
        gain = gain * one(*cut)
    return gain


def profile(count, total, limit, slope):
    loads = [(1 << 20) // math.isqrt(rank ** slope) + 1 for rank in range(2, count + 1)]
    rest, counts = total - limit - (count - 1), [1] * (count - 1)
    while rest > 0:
        movable = [i for i in range(count - 1) if counts[i] < limit]
        whole, budget = sum([loads[i] for i in movable]), rest
        for i in movable:
            extra = min(limit - counts[i], max(1, budget * loads[i] // whole), rest)
            counts[i] = counts[i] + extra
            rest = rest - extra
    return np.array([limit] + counts)


def ragged_sizes(rng, number_of, total, reach, lean):
    if number_of == 2:
        one = jax.random.randint(rng, (), max(1, total - reach), min(reach, total - 1) + 1)
        return jnp.stack([one, total - one])
    sizes = jnp.asarray(profile(number_of, total, reach, lean), jnp.int32)
    couples = (number_of - 1) // 2
    giver, receiver = sizes[1:1 + 2 * couples:2], sizes[2:2 + 2 * couples:2]
    margin = jnp.minimum(giver - 1, reach - receiver)
    shifted = jax.random.randint(jax.random.fold_in(rng, 1), (couples,), 0, 1 << 20) % (margin + 1)
    sizes = sizes.at[1:1 + 2 * couples:2].set(giver - shifted).at[2:2 + 2 * couples:2].set(receiver + shifted)
    return sizes[jax.random.permutation(jax.random.fold_in(rng, 2), number_of)]


def noise(own_key, shape, spread, reach, cuts=(), held_as=jnp.bfloat16):
    values = spread * jax.random.normal(own_key, shape, jnp.float32)
    if cuts:
        values = values * level_of(own_key, shape, cuts, -0.22, 0.18)
    return jnp.clip(values, -reach, reach).astype(held_as)


def setup_inputs(seed: int = 0) -> dict:
    streams_of = jax.random.split(jax.random.key(seed), 16)
    tokens = noise(streams_of[0], (TOKENS, D), 1.0, 6.0, ((0, 128),))
    block_table = draw_block_table(jax.random.fold_in(streams_of[15], 71), 0)
    doc_ids = jax.vmap(lambda own: jnp.searchsorted(jnp.cumsum(ragged_sizes(own, 4, LENGTH, LENGTH // 2, 1)), jnp.arange(LENGTH), side="right"))(jax.random.split(streams_of[2], SEQS)).reshape((SEQS, LENGTH)).astype(jnp.int32)
    attn_gain = jnp.clip(1.0 + 0.15 * jax.random.normal(streams_of[3], (D,), jnp.float32), 0.25, 1.75).astype(jnp.bfloat16)
    w_query = noise(streams_of[4], (D, H * HD), D ** -0.5, 0.1875, ((0, 16), (1, 8)))
    w_key = noise(streams_of[5], (D, KV * HD), D ** -0.5, 0.1875, ((0, 16), (1, 8)))
    w_value = noise(streams_of[6], (D, KV * HD), D ** -0.5, 0.1875, ((0, 16), (1, 8)))
    query_gain = jnp.clip(1.0 + 0.15 * jax.random.normal(streams_of[7], (HD,), jnp.float32), 0.25, 1.75).astype(jnp.bfloat16)
    key_gain = jnp.clip(1.0 + 0.15 * jax.random.normal(streams_of[8], (HD,), jnp.float32), 0.25, 1.75).astype(jnp.bfloat16)
    w_out = noise(streams_of[9], (H * HD, D), (H * HD // 64) ** -0.5, 1.0, ((0, 8), (1, 16)))
    ffn_gain = jnp.clip(1.0 + 0.15 * jax.random.normal(streams_of[10], (D,), jnp.float32), 0.25, 1.75).astype(jnp.bfloat16)
    w_gate = noise(streams_of[11], (D, FF), D ** -0.5, 0.1875, ((0, 16), (1, 8)))
    w_up = noise(streams_of[12], (D, FF), D ** -0.5, 0.1875, ((0, 16), (1, 8)))
    w_down = noise(streams_of[13], (FF, D), FF ** -0.5, 0.109375, ((0, 8), (1, 16)))
    out_grad = noise(streams_of[14], (TOKENS, D), 1.0, 6.0, ((0, 128),))
    return dict(tokens=tokens, block_table=block_table, doc_ids=doc_ids, attn_gain=attn_gain, w_query=w_query, w_key=w_key, w_value=w_value, query_gain=query_gain, key_gain=key_gain, w_out=w_out, ffn_gain=ffn_gain, w_gate=w_gate, w_up=w_up, w_down=w_down, out_grad=out_grad)


EPS = 1e-06
THETA = 1000000.0
HIGH = lax.Precision.HIGHEST

@jax.custom_vjp
def low(v):
    return lax.optimization_barrier(v.astype(jnp.bfloat16)).astype(jnp.float32)

@jax.custom_vjp
def low_back(v):
    return v

def low_keep(v):
    return (low(v), None)

def low_pass(kept, grad):
    return (grad,)

def back_keep(v):
    return (v, None)

def back_low(kept, grad):
    return (low(grad),)
low.defvjp(low_keep, low_pass)
low_back.defvjp(back_keep, back_low)

def matmul(left_side, right_side):
    return jnp.dot(left_side, right_side, precision=HIGH, preferred_element_type=jnp.float32)

def normed(values, norm_gain):
    return values * lax.rsqrt(lax.optimization_barrier(jnp.mean(values * values, axis=-1, keepdims=True)) + EPS) * norm_gain

def rotate(values, cos_table, sin_table):
    half_width = values.shape[-1] // 2
    turned = jnp.concatenate([-values[..., half_width:], values[..., :half_width]], axis=-1)
    return values * cos_table + turned * sin_table

def rope_tables(positions):
    freq_steps = jnp.arange(HD // 2, dtype=jnp.float32) * (2.0 / HD)
    frequency = jnp.power(jnp.float32(THETA), -freq_steps)
    angles = positions.astype(jnp.float32)[:, None] * frequency[None, :]
    angles = jnp.concatenate([angles, angles], axis=1)[:, None, :]
    return (jnp.cos(angles), jnp.sin(angles))

def one_sequence(seq_tokens, documents, positions, attn_gain, w_query, w_key, w_value, query_gain, key_gain, w_out, ffn_gain, w_gate, w_up, w_down):
    group_size = H // KV
    query_block = math.gcd(LENGTH, 512)
    cos_table, sin_table = rope_tables(positions)
    norm_one = low(normed(seq_tokens, attn_gain))
    query_pre = low_back(matmul(norm_one, w_query)).reshape(LENGTH, H, HD)
    key_pre = low_back(matmul(norm_one, w_key)).reshape(LENGTH, KV, HD)
    values = low(low_back(matmul(norm_one, w_value))).reshape(LENGTH, KV, HD)
    queries = low(rotate(normed(query_pre, query_gain), cos_table, sin_table)).reshape(LENGTH, KV, group_size, HD)
    keys_all = low(rotate(normed(key_pre, key_gain), cos_table, sin_table))
    key_index = jnp.arange(LENGTH, dtype=jnp.int32)

    def attend(first_row):
        rows_here = lax.dynamic_slice_in_dim(queries, first_row, query_block, 0)
        row_index = first_row + jnp.arange(query_block, dtype=jnp.int32)
        row_docs = lax.dynamic_slice_in_dim(documents, first_row, query_block, 0)
        scores = low_back(jnp.einsum('qhgd,khd->hgqk', rows_here, keys_all, precision=HIGH) * HD ** (-0.5))
        allowed = (key_index[None, :] <= row_index[:, None]) & (documents[None, :] == row_docs[:, None])
        scores = jnp.where(allowed, scores, -1e+30)
        probs = jax.nn.softmax(scores, axis=-1)
        return jnp.einsum('hgqk,khd->qhgd', low(probs), values, precision=HIGH)
    block_starts = jnp.arange(0, LENGTH, query_block, dtype=jnp.int32)
    attended = lax.map(jax.checkpoint(attend), block_starts).reshape(LENGTH, H * HD)
    attended = low(low_back(attended))
    resid = seq_tokens + low_back(matmul(attended, w_out))
    norm_two = low(normed(resid, ffn_gain))
    gate = low_back(matmul(norm_two, w_gate))
    up_proj = low_back(matmul(norm_two, w_up))
    act_low = low(jax.nn.silu(gate) * up_proj)
    return resid + low_back(matmul(act_low, w_down))

def reference(tokens, block_table, doc_ids, attn_gain, w_query, w_key, w_value, query_gain, key_gain, w_out, ffn_gain, w_gate, w_up, w_down, out_grad):
    row_ids = jnp.arange(TOKENS, dtype=jnp.int32)
    device = row_ids // LOCAL
    inner_row = row_ids % LOCAL
    seq_number = inner_row // (2 * BLK)
    half_index = inner_row // BLK % 2
    position = block_table[device, half_index] * BLK + inner_row % BLK
    natural = (seq_number * LENGTH + position).astype(jnp.int32)
    ordering = jnp.zeros((TOKENS,), jnp.int32).at[natural].set(row_ids)
    seq_index = jnp.arange(LENGTH, dtype=jnp.int32)
    change = jnp.concatenate([jnp.ones((SEQS, 1), dtype=bool), doc_ids[:, 1:] != doc_ids[:, :-1]], axis=1)
    doc_starts = lax.cummax(jnp.where(change, seq_index[None, :], 0), axis=1)
    positions = (seq_index[None, :] - doc_starts).astype(jnp.int32)

    def layer(flat_tokens, attn_g, w_q, w_k, w_v, query_g, key_g, w_o, ffn_g, w_g, w_u, w_d):
        seqs_in = flat_tokens[ordering].reshape(SEQS, LENGTH, D)

        def run_one(sequence_items):
            return one_sequence(sequence_items[0], sequence_items[1], sequence_items[2], attn_g, w_q, w_k, w_v, query_g, key_g, w_o, ffn_g, w_g, w_u, w_d)
        results = lax.map(run_one, (seqs_in, doc_ids, positions))
        return results.reshape(TOKENS, D)[natural]
    result, pullback = jax.vjp(layer, tokens.astype(jnp.float32), attn_gain.astype(jnp.float32), w_query.astype(jnp.float32), w_key.astype(jnp.float32), w_value.astype(jnp.float32), query_gain.astype(jnp.float32), key_gain.astype(jnp.float32), w_out.astype(jnp.float32), ffn_gain.astype(jnp.float32), w_gate.astype(jnp.float32), w_up.astype(jnp.float32), w_down.astype(jnp.float32))
    grads = pullback(out_grad.astype(jnp.float32))
    return (result.astype(jnp.bfloat16), grads[0].astype(jnp.bfloat16), grads[1], grads[2], grads[3], grads[4], grads[5], grads[6], grads[7], grads[8], grads[9], grads[10], grads[11])
```

```python
import functools
import math

import jax
import jax.numpy as jnp
from jax import lax
from jax.experimental import pallas as pl
from jax.experimental.pallas import tpu as pltpu
from jax.sharding import PartitionSpec as P

HD = 128
BLK = 128
EPS = 1e-06
THETA = 1000000.0
SCALE = HD ** (-0.5)
LOG2E = math.log2(math.e)
LN2 = math.log(2.0)
BF = jnp.bfloat16
F32 = jnp.float32
ALL = ("ctx", "tp")
RING = (0, 1, 3, 2)
ROWS = 1024
KEYS = 4096
FWD_KEYS = 512
BWD_KEYS = 512
VMEM = pltpu.CompilerParams(vmem_limit_bytes=48 * 1024 * 1024)


def cost(us):
    return pl.CostEstimate(flops=int(us * 1e9), bytes_accessed=int(us * 1e6), transcendentals=0)


def place_of(x, y, z, core):
    x, y, z, core = x % 4, y % 4, z % 4, core % 2
    return (((x % 2) * 4 + z) * 2 + core) * 8 + y * 2 + x // 2


def all_places():
    return [(x, y, z, c) for x in range(4) for y in range(4) for z in range(4) for c in range(2)]


def shift(value, dx=0, dy=0, dz=0, dcore=0):
    pairs = [
        (place_of(x, y, z, c), place_of(x + dx, y + dy, z + dz, c + dcore)) for x, y, z, c in all_places()
    ]
    return lax.ppermute(value, ALL, pairs)


def weight_pairs(step):
    pairs = []
    for x, y, z, c in all_places():
        pairs.append(
            (place_of(x, y, z, c), place_of((x // 2) * 2 + y // 2, (2 * (x % 2) + c + step) % 4, z, y % 2))
        )
    return pairs


def contract_last(left_side, right_side):
    return lax.dot_general(left_side, right_side, (((1,), (1,)), ((), ())), preferred_element_type=F32)


def contract_first(left_side, right_side):
    return lax.dot_general(left_side, right_side, (((0,), (0,)), ((), ())), preferred_element_type=F32)


def dot(left_side, right_side):
    return jnp.dot(left_side, right_side, preferred_element_type=F32)


def gather_rows(own):
    half = jnp.concatenate([own] + [shift(own, dx=-d) for d in RING[1:]], axis=0)
    return jnp.concatenate([half, shift(half, dcore=1)], axis=0)


def reduce_rows(partial_low):
    half = partial_low.shape[0] // 2
    got = shift(partial_low[half:], dcore=1)
    both = (partial_low[:half].astype(F32) + got.astype(F32)).astype(BF)
    rows = half // 4
    total = both[:rows].astype(F32)
    arrived = [shift(both[k * rows : (k + 1) * rows], dx=RING[k]) for k in range(1, 4)]
    for part in arrived:
        total = total + part.astype(F32)
    return total


def after(values, *others):
    return lax.optimization_barrier((values, others))[0]


def assemble_kernel(widths, offs_ref, *refs):
    slots, outs = refs[:4], refs[4:]
    for s in range(4):
        for k in range(4):
            rows = pl.ds(pl.multiple_of(offs_ref[s * 4 + k], 64), 64)
            col = 0
            for out, width in zip(outs, widths, strict=True):
                out[rows, :] = slots[s][k * 64 : (k + 1) * 64, col : col + width]
                col += width


def to_users(shard):
    return jnp.concatenate([lax.ppermute(shard, ALL, weight_pairs(step)) for step in range(4)], axis=0)


def along_z(mine):
    return [mine] + [shift(mine, dz=-d) for d in RING[1:]]


def assembled(slots, widths, offs):
    vmem = pl.BlockSpec(memory_space=pltpu.VMEM)
    return pl.pallas_call(
        functools.partial(assemble_kernel, widths),
        out_shape=[jax.ShapeDtypeStruct((ROWS, w), BF) for w in widths],
        in_specs=[pl.BlockSpec(memory_space=pltpu.SMEM)] + [vmem] * 4,
        out_specs=[vmem] * len(widths),
        compiler_params=VMEM,
        cost_estimate=cost(1 + sum(widths) / 512),
        name="assemble",
    )(offs, *slots)


def sum_ring(value, axis):
    arrived = [shift(value, **{axis: d}) for d in RING[1:]]
    return value + arrived[0] + (arrived[1] + arrived[2])


def reduce_along_z(grads, z):
    width = grads.shape[1]
    parts = grads.astype(BF).reshape(2, 4, 2, 64, width)

    def rows_for(d):
        return lax.dynamic_index_in_dim(parts, (z + d) % 4, 1, keepdims=False)

    total = rows_for(0).astype(F32)
    arrived = [shift(rows_for(d), dz=d) for d in RING[1:]]
    for part in arrived:
        total = total + part.astype(F32)
    return total.astype(BF).reshape(4, 64, width)


def to_owners(low, y):
    result = None
    for step in range(4):
        piece = lax.dynamic_index_in_dim(low, (y - step) % 4, 0, keepdims=False)
        back = [(b, a) for a, b in weight_pairs(step)]
        got = lax.ppermute(piece, ALL, back).astype(F32)
        result = got if result is None else result + got
    return result


def head_norm(pre):
    return pre * lax.rsqrt(jnp.mean(pre * pre, axis=-1, keepdims=True) + EPS)


def qkv_kernel(tok_ref, gain_ref, w_ref, qg_ref, kg_ref, cos_ref, sin_ref, norm_ref, q_ref, kv_ref, pre_ref):
    tok = tok_ref[...].astype(F32)
    rate = lax.rsqrt(jnp.mean(tok * tok, axis=-1, keepdims=True) + EPS)
    low = (tok * rate * gain_ref[...]).astype(BF)
    norm_ref[...] = low
    proj = dot(low, w_ref[...])
    cos, sin = cos_ref[...], sin_ref[...]
    pre_ref[...] = proj[:, : 3 * HD]
    for h in range(3):
        gain = qg_ref[...] if h < 2 else kg_ref[...]
        u = head_norm(proj[:, h * HD : (h + 1) * HD]) * gain
        u = u * cos + pltpu.roll(u, HD // 2, 1) * sin
        if h < 2:
            q_ref[:, h * HD : (h + 1) * HD] = (u * (SCALE * LOG2E)).astype(BF)
        else:
            kv_ref[:, :HD] = u.astype(BF)
    kv_ref[:, HD:] = proj[:, 3 * HD :].astype(BF)


def project(tokens, gain, w_qkv, q_gain, k_gain, cos, sin):
    rows, d = tokens.shape
    step = 256
    by_rows = lambda w: pl.BlockSpec((step, w), lambda i: (i, 0))
    whole = lambda a: pl.BlockSpec(a.shape, lambda i: (0, 0))
    return pl.pallas_call(
        qkv_kernel,
        grid=(rows // step,),
        in_specs=[by_rows(d), whole(gain), whole(w_qkv), whole(q_gain), whole(k_gain), by_rows(HD), by_rows(HD)],
        out_specs=[by_rows(d), by_rows(2 * HD), by_rows(2 * HD), by_rows(3 * HD)],
        out_shape=[
            jax.ShapeDtypeStruct((rows, d), BF),
            jax.ShapeDtypeStruct((rows, 2 * HD), BF),
            jax.ShapeDtypeStruct((rows, 2 * HD), BF),
            jax.ShapeDtypeStruct((rows, 3 * HD), F32),
        ],
        compiler_params=VMEM,
        cost_estimate=cost(5),
        name="project",
    )(tokens, gain, w_qkv, q_gain, k_gain, cos, sin)


def qkv_back_kernel(
    dq_ref, kv0, kv1, kv2, kv3, pre_ref, cos_ref, sin_ref, qg_ref, kg_ref, tok_ref, w_ref,
    gqkv_ref, gnorm_ref, gattn_ref, gq_ref, gk_ref,
):
    @pl.when(pl.program_id(0) == 0)
    def _():
        gattn_ref[...] = jnp.zeros_like(gattn_ref)
        gq_ref[...] = jnp.zeros_like(gq_ref)
        gk_ref[...] = jnp.zeros_like(gk_ref)

    dkv = kv0[...].astype(F32) + kv1[...].astype(F32) + kv2[...].astype(F32) + kv3[...].astype(F32)
    cos, sin = cos_ref[...], sin_ref[...]
    for h in range(3):
        grad = dq_ref[:, h * HD : (h + 1) * HD] if h < 2 else dkv[:, :HD]
        gain = qg_ref[...] if h < 2 else kg_ref[...]
        u = pre_ref[:, h * HD : (h + 1) * HD]
        rate = lax.rsqrt(jnp.mean(u * u, axis=-1, keepdims=True) + EPS)
        n = u * rate
        g = grad * cos - pltpu.roll(grad, HD // 2, 1) * sin
        gained = gain * g
        pre_grad = (gained - n * jnp.mean(gained * n, axis=-1, keepdims=True)) * rate
        gqkv_ref[:, h * HD : (h + 1) * HD] = pre_grad.astype(BF)
        sums = jnp.sum((g * n).reshape(-1, 8, HD), axis=0)
        if h < 2:
            gq_ref[...] += sums
        else:
            gk_ref[...] += sums
    gqkv_ref[:, 3 * HD :] = dkv[:, HD:].astype(BF)
    gnorm = contract_last(gqkv_ref[...], w_ref[...])
    gnorm_ref[...] = gnorm.astype(BF)
    tok = tok_ref[...].astype(F32)
    xhat = tok * lax.rsqrt(jnp.mean(tok * tok, axis=-1, keepdims=True) + EPS)
    gattn_ref[...] += jnp.sum((gnorm * xhat).reshape(-1, 8, gnorm.shape[1]), axis=0)


def project_back(dq, dkv, pre, cos, sin, q_gain, k_gain, tokens, w_qkv):
    rows, d = tokens.shape
    step = 256
    by_rows = lambda w: pl.BlockSpec((step, w), lambda i: (i, 0))
    whole = lambda a: pl.BlockSpec(a.shape, lambda i: (0, 0))
    fixed = lambda w: pl.BlockSpec((8, w), lambda i: (0, 0))
    return pl.pallas_call(
        qkv_back_kernel,
        grid=(rows // step,),
        in_specs=[by_rows(2 * HD)]
        + [by_rows(2 * HD)] * 4
        + [by_rows(3 * HD), by_rows(HD), by_rows(HD), whole(q_gain), whole(k_gain), by_rows(d), whole(w_qkv)],
        out_specs=[by_rows(4 * HD), by_rows(d), fixed(d), fixed(HD), fixed(HD)],
        out_shape=[
            jax.ShapeDtypeStruct((rows, 4 * HD), BF),
            jax.ShapeDtypeStruct((rows, d), BF),
            jax.ShapeDtypeStruct((8, d), F32),
            jax.ShapeDtypeStruct((8, HD), F32),
            jax.ShapeDtypeStruct((8, HD), F32),
        ],
        compiler_params=VMEM,
        cost_estimate=cost(9),
        name="project_back",
    )(dq, *dkv, pre, cos, sin, q_gain, k_gain, tokens, w_qkv)


def stacked(ref, i):
    rows = ref[pl.ds(pl.multiple_of(i * BLK, BLK), BLK), :]
    return jnp.concatenate([rows[:, :HD], rows[:, HD:]], axis=0)


def allowed_keys(start, place, first, count):
    pos = first + lax.broadcasted_iota(jnp.int32, (count, 2 * BLK), 0)
    return (pos >= start) & (pos <= place)


def query_places(qblk):
    lane = lax.broadcasted_iota(jnp.int32, (1, 2 * BLK), 1)
    return qblk * BLK + (lane & (BLK - 1))


def attend_kernel(kblk, qblk, low, start_ref, q_ref, kv0, kv1, kv2, kv3, out_ref, o_ref, lse_ref, keys, values_t):
    for s, ref in enumerate((kv0, kv1, kv2, kv3)):
        for j in range(8):
            at = pl.multiple_of(kblk[s * 8 + j] * BLK, BLK)
            keys[pl.ds(at, BLK), :] = ref[j * BLK : (j + 1) * BLK, :HD]
            values_t[:, pl.ds(at, BLK)] = ref[j * BLK : (j + 1) * BLK, HD:].T
    chunk = FWD_KEYS // BLK

    def one_block(i, _):
        q = stacked(q_ref, i)
        start = start_ref[i]
        place = query_places(qblk[i])

        def one_chunk(c, carry):
            acc, total = carry
            first = pl.multiple_of(c * FWD_KEYS, FWD_KEYS)
            scores = contract_last(keys[pl.ds(first, FWD_KEYS), :], q)
            ok = allowed_keys(start, place, first, FWD_KEYS)
            weights = jnp.where(ok, jnp.exp2(scores), 0.0)
            total = total + jnp.sum(weights.reshape(-1, 8, 2 * BLK), axis=0)
            acc = acc + dot(values_t[:, pl.ds(first, FWD_KEYS)], weights.astype(BF))
            return acc, total

        acc, total = lax.fori_loop(
            low[i] // chunk,
            qblk[i] // chunk + 1,
            one_chunk,
            (jnp.zeros((HD, 2 * BLK), F32), jnp.zeros((8, 2 * BLK), F32)),
        )
        total = jnp.sum(total, axis=0, keepdims=True)
        o = acc * (1.0 / total)
        o_ref[i] = o
        lse_ref[i] = jnp.log2(total)
        rows = o.T.astype(BF)
        out_ref[pl.ds(pl.multiple_of(i * BLK, BLK), BLK), :] = jnp.concatenate([rows[:BLK], rows[BLK:]], axis=1)
        return 0

    lax.fori_loop(0, ROWS // BLK, one_block, 0)


def attend(kblk, qblk, low, start, q, kv):
    smem = pl.BlockSpec(memory_space=pltpu.SMEM)
    vmem = pl.BlockSpec(memory_space=pltpu.VMEM)
    blocks = ROWS // BLK
    return pl.pallas_call(
        attend_kernel,
        in_specs=[smem] * 3 + [vmem] * 6,
        out_specs=[vmem] * 3,
        out_shape=[
            jax.ShapeDtypeStruct((ROWS, 2 * HD), BF),
            jax.ShapeDtypeStruct((blocks, HD, 2 * BLK), F32),
            jax.ShapeDtypeStruct((blocks, 1, 2 * BLK), F32),
        ],
        scratch_shapes=[pltpu.VMEM((KEYS, HD), BF), pltpu.VMEM((HD, KEYS), BF)],
        compiler_params=VMEM,
        cost_estimate=cost(14),
        name="attend",
    )(kblk, qblk, low, start, q, *kv)


def attend_back_kernel(
    kblk, qblk, low, start_ref, q_ref, do_ref, o_ref, lse_ref, kv0, kv1, kv2, kv3,
    dq_ref, dkv0, dkv1, dkv2, dkv3, keys, keys_t, values, dk, dv,
):
    for s, ref in enumerate((kv0, kv1, kv2, kv3)):
        for j in range(8):
            at = pl.multiple_of(kblk[s * 8 + j] * BLK, BLK)
            key = ref[j * BLK : (j + 1) * BLK, :HD]
            keys[pl.ds(at, BLK), :] = key
            keys_t[:, pl.ds(at, BLK)] = key.T
            values[pl.ds(at, BLK), :] = ref[j * BLK : (j + 1) * BLK, HD:]
    dk[...] = jnp.zeros_like(dk)
    dv[...] = jnp.zeros_like(dv)
    chunk = BWD_KEYS // BLK

    def one_block(i, _):
        q = stacked(q_ref, i)
        do = stacked(do_ref, i)
        delta = jnp.sum(do.astype(F32).T * o_ref[i], axis=0, keepdims=True)
        lse = lse_ref[i]
        start = start_ref[i]
        place = query_places(qblk[i])

        def one_chunk(c, acc):
            first = pl.multiple_of(c * BWD_KEYS, BWD_KEYS)
            here = pl.ds(first, BWD_KEYS)
            scores = contract_last(keys[here, :], q)
            ok = allowed_keys(start, place, first, BWD_KEYS)
            probs = jnp.where(ok, jnp.exp2(scores - lse), 0.0)
            dprobs = contract_last(values[here, :], do)
            dscores = (probs * (dprobs - delta)).astype(BF)
            dv[here, :] += dot(probs.astype(BF), do)
            dk[here, :] += dot(dscores, q)
            return acc + dot(keys_t[:, here], dscores)

        acc = lax.fori_loop(low[i] // chunk, qblk[i] // chunk + 1, one_chunk, jnp.zeros((HD, 2 * BLK), F32))
        rows = acc.T * SCALE
        dq_ref[pl.ds(pl.multiple_of(i * BLK, BLK), BLK), :] = jnp.concatenate([rows[:BLK], rows[BLK:]], axis=1)
        return 0

    lax.fori_loop(0, ROWS // BLK, one_block, 0)
    for s, ref in enumerate((dkv0, dkv1, dkv2, dkv3)):
        for j in range(8):
            at = pl.multiple_of(kblk[s * 8 + j] * BLK, BLK)
            ref[j * BLK : (j + 1) * BLK, :HD] = (dk[pl.ds(at, BLK), :] * LN2).astype(BF)
            ref[j * BLK : (j + 1) * BLK, HD:] = dv[pl.ds(at, BLK), :].astype(BF)


def attend_back(kblk, qblk, low, start, q, do, o, lse, kv):
    smem = pl.BlockSpec(memory_space=pltpu.SMEM)
    vmem = pl.BlockSpec(memory_space=pltpu.VMEM)
    return pl.pallas_call(
        attend_back_kernel,
        in_specs=[smem] * 3 + [vmem] * 9,
        out_specs=[vmem] * 5,
        out_shape=[jax.ShapeDtypeStruct((ROWS, 2 * HD), F32)] + [jax.ShapeDtypeStruct((ROWS, 2 * HD), BF)] * 4,
        scratch_shapes=[
            pltpu.VMEM((KEYS, HD), BF),
            pltpu.VMEM((HD, KEYS), BF),
            pltpu.VMEM((KEYS, HD), BF),
            pltpu.VMEM((KEYS, HD), F32),
            pltpu.VMEM((KEYS, HD), F32),
        ],
        compiler_params=VMEM,
        cost_estimate=cost(20),
        name="attend_back",
    )(kblk, qblk, low, start, q, do, o, lse, *kv)


def per_device(
    tokens,
    block_table,
    doc_ids,
    attn_gain,
    w_query,
    w_key,
    w_value,
    query_gain,
    key_gain,
    w_out,
    ffn_gain,
    w_gate,
    w_up,
    w_down,
    out_grad,
):
    ctx_rank = lax.axis_index("ctx")
    tp_rank = lax.axis_index("tp")
    x_lo, z, core = ctx_rank // 8, (ctx_rank // 2) % 4, ctx_rank % 2
    y, x_hi = tp_rank // 2, tp_rank % 2
    x = 2 * x_hi + x_lo
    d_model = tokens.shape[1]
    q_width, k_width, ff_local = w_query.shape[1], w_key.shape[1], w_gate.shape[1]

    ring = jnp.array(RING, jnp.int32)
    xs = ((x + ring) % 4)[None, None, :]
    zs = ((z + ring) % 4)[:, None, None]
    cores = ((core + jnp.arange(2, dtype=jnp.int32)) % 2)[None, :, None]
    entry = ((((xs % 2) * 4 + zs) * 2 + cores) * 2 + xs // 2).reshape(32)
    table = block_table.reshape(32)
    kblk = jnp.sum(
        jnp.where(entry[:, None] == jnp.arange(32, dtype=jnp.int32)[None, :], table[None, :], 0), axis=1
    ).astype(jnp.int32)
    qblk = kblk[:8]
    docs = lax.dynamic_index_in_dim(doc_ids, y, 0, keepdims=False)
    firsts = jnp.sum((docs[None, :] < jnp.arange(4, dtype=jnp.int32)[:, None]).astype(jnp.int32), axis=1)
    place = qblk[:, None] * BLK + jnp.arange(BLK, dtype=jnp.int32)[None, :]
    start = jnp.max(
        jnp.where(firsts[:, None, None] <= place[None], firsts[:, None, None], 0), axis=0
    )
    low = start[:, 0] // BLK
    start2 = jnp.concatenate([start, start], axis=1)[:, None, :]
    pos = (place - start).reshape(ROWS)
    freq = jnp.power(jnp.float32(THETA), -(jnp.arange(HD // 2, dtype=F32) * (2.0 / HD)))
    angles = pos.astype(F32)[:, None] * freq[None, :]
    cos_half, sin_half = jnp.cos(angles), jnp.sin(angles)
    cos = jnp.concatenate([cos_half, cos_half], axis=1)
    sin = jnp.concatenate([-sin_half, sin_half], axis=1)
    bits = ((y - jnp.arange(4, dtype=jnp.int32)) % 4)[None, :]
    offs = (((bits // 2) * 4 + zs.reshape(4, 1)) * 2 + bits % 2).reshape(16) * 64

    def head_gain(gain):
        return jnp.concatenate([gain, jnp.zeros((64 - gain.shape[0],), BF)])

    gains = jnp.stack([attn_gain, ffn_gain, head_gain(query_gain), head_gain(key_gain)], axis=1)
    gains = jnp.concatenate([gains, jnp.zeros((64, 124), BF)], axis=1)
    w_o, w_d = w_out.shape[0], w_down.shape[0]
    first_mine = to_users(jnp.concatenate([w_query, w_key, w_value, gains], axis=1))
    w_qkv, gain_cols = assembled(along_z(first_mine), (q_width + 2 * k_width, 128), offs)
    second_shard = jnp.concatenate([w_out.T, w_gate, w_up, w_down.T], axis=1)
    second_mine = to_users(after(second_shard, first_mine))
    gain_rows = gain_cols[:, :8].astype(F32).T
    gain_attn, gain_ffn = gain_rows[0:1], gain_rows[1:2]
    gain_query = gain_rows[2].reshape(16, 64)[:, :8].reshape(1, HD)
    gain_key = gain_rows[3].reshape(16, 64)[:, :8].reshape(1, HD)

    rows_tok = gather_rows(tokens)
    rows_tok = after(rows_tok, second_mine)
    normal_one, q, kv, pre = project(rows_tok, gain_attn, w_qkv, gain_query, gain_key, cos, sin)
    kv_all = along_z(kv)
    grad_rows = gather_rows(after(out_grad, kv))
    out_mine, ffn_mine = after((second_mine[:, :w_o], second_mine[:, w_o:]), *kv_all)
    out_slots = along_z(out_mine)
    attn_low, o, lse = attend(kblk, qblk, low, start2, q, kv_all)
    (w_proj,) = assembled(out_slots, (w_o,), offs)
    w_gu, w_dn = assembled(along_z(after(ffn_mine, *out_slots)), (2 * ff_local, w_d), offs)
    grad_rows = after(grad_rows, attn_low)
    resid = tokens.astype(F32) + reduce_rows(contract_last(attn_low, w_proj).astype(BF))
    rate_two = lax.rsqrt(jnp.mean(resid * resid, axis=-1, keepdims=True) + EPS)
    xhat_two = resid * rate_two
    rows_two = gather_rows((xhat_two * gain_ffn).astype(BF))
    gate_up = dot(rows_two, w_gu)
    gate, up_proj = gate_up[:, :ff_local], gate_up[:, ff_local:]
    sigmoid_gate = jax.nn.sigmoid(gate)
    silu_gate = gate * sigmoid_gate
    hidden = (silu_gate * up_proj).astype(BF)
    grad_hidden = dot(grad_rows, w_dn)
    grad_gate = grad_hidden * up_proj * (sigmoid_gate * (1.0 + gate * (1.0 - sigmoid_gate)))
    grad_up = grad_hidden * silu_gate
    grad_gu = jnp.concatenate([grad_gate, grad_up], axis=1).astype(BF)
    grad_norm_two = reduce_rows(contract_last(grad_gu, w_gu).astype(BF))
    ffn_low = reduce_along_z(
        jnp.concatenate([contract_first(rows_two, grad_gu), contract_first(grad_rows, hidden)], axis=1), z
    )
    grad_gain_ffn = jnp.sum(grad_norm_two * xhat_two, axis=0)
    gained = grad_norm_two * gain_ffn
    grad_resid = out_grad.astype(F32) + (
        gained - xhat_two * jnp.mean(gained * xhat_two, axis=-1, keepdims=True)
    ) * rate_two
    branch_rows = gather_rows(grad_resid.astype(BF))
    grad_attn = dot(branch_rows, w_proj).astype(BF)
    grad_attn, ffn_low = lax.optimization_barrier((grad_attn, ffn_low))
    out_low = reduce_along_z(contract_first(branch_rows, attn_low), z)
    out = (resid + reduce_rows(after(contract_last(hidden, w_dn).astype(BF), branch_rows))).astype(BF)

    dq, *dkv = attend_back(kblk, qblk, low, start2, q, grad_attn, o, lse, kv_all)
    dkv_all = [dkv[0]] + [shift(dkv[k], dz=RING[k]) for k in range(1, 4)]
    late_owned = to_owners(jnp.concatenate([out_low, ffn_low], axis=2), y)
    dq, out, late_owned = lax.optimization_barrier((dq, out, late_owned))
    grad_qkv, grad_one, sum_attn, sum_query, sum_key = project_back(
        dq, dkv_all, pre, cos, sin, gain_query, gain_key, rows_tok, w_qkv
    )
    grad_norm_one = reduce_rows(grad_one)
    tok = tokens.astype(F32)
    rate_one = lax.rsqrt(jnp.mean(tok * tok, axis=-1, keepdims=True) + EPS)
    xhat_one = tok * rate_one
    gained = grad_norm_one * gain_attn
    grad_x = (
        grad_resid + (gained - xhat_one * jnp.mean(gained * xhat_one, axis=-1, keepdims=True)) * rate_one
    ).astype(BF)
    qkv_owned = to_owners(reduce_along_z(contract_first(normal_one, grad_qkv), z), y)
    sums = jnp.concatenate(
        [jnp.sum(sum_attn, axis=0), grad_gain_ffn, jnp.sum(sum_query, axis=0), jnp.sum(sum_key, axis=0)]
    )
    sums = sums + shift(sums, dcore=1)
    for axis in ("dx", "dz", "dy"):
        sums = sum_ring(sums, axis)
    share = d_model // 16

    def own_part(first, size):
        return lax.dynamic_slice_in_dim(sums, first + ctx_rank * size, size)

    return (
        out,
        grad_x,
        own_part(0, share),
        qkv_owned[:, :q_width],
        qkv_owned[:, q_width : q_width + k_width],
        qkv_owned[:, q_width + k_width :],
        own_part(2 * d_model, HD // 16),
        own_part(2 * d_model + HD, HD // 16),
        late_owned[:, :w_o].T,
        own_part(d_model, share),
        late_owned[:, w_o : w_o + ff_local],
        late_owned[:, w_o + ff_local : w_o + 2 * ff_local],
        late_owned[:, w_o + 2 * ff_local :].T,
    )


def solution(mesh):
    in_specs = (
        P(("ctx", "tp"), None),
        P(),
        P(),
        P("ctx"),
        P("ctx", "tp"),
        P("ctx", "tp"),
        P("ctx", "tp"),
        P("ctx"),
        P("ctx"),
        P("tp", "ctx"),
        P("ctx"),
        P("ctx", "tp"),
        P("ctx", "tp"),
        P("tp", "ctx"),
        P(("ctx", "tp"), None),
    )
    out_specs = (
        P(("ctx", "tp"), None),
        P(("ctx", "tp"), None),
        P("ctx"),
        P("ctx", "tp"),
        P("ctx", "tp"),
        P("ctx", "tp"),
        P("ctx"),
        P("ctx"),
        P("tp", "ctx"),
        P("ctx"),
        P("ctx", "tp"),
        P("ctx", "tp"),
        P("tp", "ctx"),
    )
    return jax.shard_map(
        per_device, mesh=mesh, in_specs=in_specs, out_specs=out_specs, check_vma=False
    )
```

```python
import functools
import math

import jax
import jax.numpy as jnp
from jax import lax
from jax.experimental import pallas as pl
from jax.experimental.pallas import tpu as pltpu
from jax.sharding import PartitionSpec as P

HD = 128
BLK = 128
EPS = 1e-06
THETA = 1000000.0
SCALE = HD ** (-0.5)
LOG2E = math.log2(math.e)
LN2 = math.log(2.0)
BF = jnp.bfloat16
F32 = jnp.float32
ALL = ("ctx", "tp")
RING = (0, 1, 3, 2)
ROWS = 1024
KEYS = 4096
FWD_KEYS = 1024
BWD_KEYS = 1024
VMEM = pltpu.CompilerParams(vmem_limit_bytes=48 * 1024 * 1024)


def cost(us):
    return pl.CostEstimate(flops=int(us * 1e9), bytes_accessed=int(us * 1e6), transcendentals=0)


def place_of(x, y, z, core):
    x, y, z, core = x % 4, y % 4, z % 4, core % 2
    return (((x % 2) * 4 + z) * 2 + core) * 8 + y * 2 + x // 2


def all_places():
    return [(x, y, z, c) for x in range(4) for y in range(4) for z in range(4) for c in range(2)]


def shift(value, dx=0, dy=0, dz=0, dcore=0):
    pairs = [
        (place_of(x, y, z, c), place_of(x + dx, y + dy, z + dz, c + dcore)) for x, y, z, c in all_places()
    ]
    return lax.ppermute(value, ALL, pairs)


def weight_pairs(step):
    pairs = []
    for x, y, z, c in all_places():
        pairs.append(
            (place_of(x, y, z, c), place_of((x // 2) * 2 + y // 2, (2 * (x % 2) + c + step) % 4, z, y % 2))
        )
    return pairs


def contract_last(left_side, right_side):
    return lax.dot_general(left_side, right_side, (((1,), (1,)), ((), ())), preferred_element_type=F32)


def contract_first(left_side, right_side):
    return lax.dot_general(left_side, right_side, (((0,), (0,)), ((), ())), preferred_element_type=F32)


def dot(left_side, right_side):
    return jnp.dot(left_side, right_side, preferred_element_type=F32)


def gather_rows(own, gate=()):
    half = jnp.concatenate([own] + [shift(own, dx=-d) for d in RING[1:]], axis=0)
    half = after(half, *gate)
    return jnp.concatenate([half, shift(half, dcore=1)], axis=0)


def sum_cores(other, mine):
    got = shift(other, dcore=1)
    return mine(got.astype(F32)).astype(BF)


def to_chips(both):
    rows = both.shape[0] // 4
    return [shift(both[k * rows : (k + 1) * rows], dx=RING[k]) for k in range(1, 4)]


def summed(both, arrived):
    total = both[: both.shape[0] // 4].astype(F32)
    for part in arrived:
        total = total + part.astype(F32)
    return total


def sum_product(product, left_side, right_side):
    half = left_side.shape[0] // 2
    other = product(left_side[half:], right_side).astype(BF)
    return sum_cores(other, lambda got: product(left_side[:half], right_side) + got)


def after(values, *others):
    return lax.optimization_barrier((values, others))[0]


def assemble_kernel(widths, offs_ref, *refs):
    slots, outs = refs[:4], refs[4:]
    for s in range(4):
        for k in range(4):
            rows = pl.ds(pl.multiple_of(offs_ref[s * 4 + k], 64), 64)
            col = 0
            for out, width in zip(outs, widths, strict=True):
                out[rows, :] = slots[s][k * 64 : (k + 1) * 64, col : col + width]
                col += width


def to_users(shard):
    return [lax.ppermute(shard, ALL, weight_pairs(step)) for step in range(4)]


def along_z(mine):
    return [mine] + [shift(mine, dz=-d) for d in RING[1:]]


def assembled(slots, widths, offs):
    vmem = pl.BlockSpec(memory_space=pltpu.VMEM)
    return pl.pallas_call(
        functools.partial(assemble_kernel, widths),
        out_shape=[jax.ShapeDtypeStruct((ROWS, w), BF) for w in widths],
        in_specs=[pl.BlockSpec(memory_space=pltpu.SMEM)] + [vmem] * 4,
        out_specs=[vmem] * len(widths),
        compiler_params=VMEM,
        cost_estimate=cost(1 + sum(widths) / 512),
        name="assemble",
    )(offs, *slots)


def send_along_z(grads, z):
    parts = grads.astype(BF).reshape(2, 4, 2, -1, grads.shape[-1])

    def rows_for(d):
        return lax.dynamic_index_in_dim(parts, (z + d) % 4, 1, keepdims=False)

    return [rows_for(0)] + [shift(rows_for(d), dz=d) for d in RING[1:]]


def sum_along_z(parts):
    total = parts[0].astype(F32)
    for part in parts[1:]:
        total = total + part.astype(F32)
    return total.astype(BF).reshape(4, -1, parts[0].shape[-1])


def to_owners(low, y):
    result = None
    for step in range(4):
        piece = lax.dynamic_index_in_dim(low, (y - step) % 4, 0, keepdims=False)
        back = [(b, a) for a, b in weight_pairs(step)]
        got = lax.ppermute(piece, ALL, back).astype(F32)
        result = got if result is None else result + got
    return result


def head_norm(pre):
    return pre * lax.rsqrt(jnp.mean(pre * pre, axis=-1, keepdims=True) + EPS)


def qkv_kernel(tok_ref, gain_ref, w_ref, qg_ref, kg_ref, cos_ref, sin_ref, norm_ref, q_ref, kv_ref, pre_ref):
    tok = tok_ref[...].astype(F32)
    rate = lax.rsqrt(jnp.mean(tok * tok, axis=-1, keepdims=True) + EPS)
    low = (tok * rate * gain_ref[...]).astype(BF)
    norm_ref[...] = low
    proj = dot(low, w_ref[...])
    cos, sin = cos_ref[...], sin_ref[...]
    pre_ref[...] = proj[:, : 3 * HD]
    for h in range(3):
        gain = qg_ref[...] if h < 2 else kg_ref[...]
        u = head_norm(proj[:, h * HD : (h + 1) * HD]) * gain
        u = u * cos + pltpu.roll(u, HD // 2, 1) * sin
        if h < 2:
            q_ref[:, h * HD : (h + 1) * HD] = (u * (SCALE * LOG2E)).astype(BF)
        else:
            kv_ref[:, :HD] = u.astype(BF)
    kv_ref[:, HD:] = proj[:, 3 * HD :].astype(BF)


def project(tokens, gain, w_qkv, q_gain, k_gain, cos, sin):
    rows, d = tokens.shape
    step = 256
    by_rows = lambda w: pl.BlockSpec((step, w), lambda i: (i, 0))
    whole = lambda a: pl.BlockSpec(a.shape, lambda i: (0, 0))
    return pl.pallas_call(
        qkv_kernel,
        grid=(rows // step,),
        in_specs=[by_rows(d), whole(gain), whole(w_qkv), whole(q_gain), whole(k_gain), by_rows(HD), by_rows(HD)],
        out_specs=[by_rows(d), by_rows(2 * HD), by_rows(2 * HD), by_rows(3 * HD)],
        out_shape=[
            jax.ShapeDtypeStruct((rows, d), BF),
            jax.ShapeDtypeStruct((rows, 2 * HD), BF),
            jax.ShapeDtypeStruct((rows, 2 * HD), BF),
            jax.ShapeDtypeStruct((rows, 3 * HD), F32),
        ],
        compiler_params=VMEM,
        cost_estimate=cost(1),
        name="project",
    )(tokens, gain, w_qkv, q_gain, k_gain, cos, sin)


def qkv_back_kernel(
    dq_ref, kv0, kv1, kv2, kv3, pre_ref, cos_ref, sin_ref, qg_ref, kg_ref, tok_ref, w_ref, norm_ref, gout_ref, gffn_ref,
    gw_ref, mine_ref, other_ref, sums_ref, gw_sum,
):
    step = pl.program_id(0)

    @pl.when(step == 0)
    def _():
        sums_ref[...] = jnp.zeros_like(sums_ref)
        sums_ref[1:2, :] = gffn_ref[...]
        gw_sum[...] = jnp.zeros_like(gw_sum)

    dkv = kv0[...].astype(F32) + kv1[...].astype(F32) + kv2[...].astype(F32) + kv3[...].astype(F32)
    cos, sin = cos_ref[...], sin_ref[...]
    grads = []
    for h in range(3):
        grad = dq_ref[:, h * HD : (h + 1) * HD] if h < 2 else dkv[:, :HD]
        gain = qg_ref[...] if h < 2 else kg_ref[...]
        u = pre_ref[:, h * HD : (h + 1) * HD]
        rate = lax.rsqrt(jnp.mean(u * u, axis=-1, keepdims=True) + EPS)
        n = u * rate
        g = grad * cos - pltpu.roll(grad, HD // 2, 1) * sin
        gained = gain * g
        pre_grad = (gained - n * jnp.mean(gained * n, axis=-1, keepdims=True)) * rate
        grads.append(pre_grad.astype(BF))
        row = 2 if h < 2 else 3
        sums_ref[row : row + 1, :HD] += jnp.sum(g * n, axis=0, keepdims=True)
    gqkv = jnp.concatenate(grads + [dkv[:, HD:].astype(BF)], axis=1)
    gw_sum[...] += contract_first(norm_ref[...], gqkv)
    gnorm = contract_last(gqkv, w_ref[...])

    @pl.when(step < 2)
    def _():
        other_ref[...] = gnorm.astype(BF)

    @pl.when(step >= 2)
    def _():
        mine_ref[...] = gnorm.astype(BF)

    tok = tok_ref[...].astype(F32)
    xhat = tok * lax.rsqrt(jnp.mean(tok * tok, axis=-1, keepdims=True) + EPS)
    sums_ref[0:1, :] += jnp.sum(gnorm * xhat, axis=0, keepdims=True)

    @pl.when(step == 3)
    def _():
        gw_ref[:, : 4 * HD] = gw_sum[...].astype(BF)
        gw_ref[:, 4 * HD :] = gout_ref[...]


def project_back(dq, dkv, pre, cos, sin, q_gain, k_gain, tokens, w_qkv, norm, grad_out, grad_gain_ffn):
    rows, d = tokens.shape
    step = 256
    by_rows = lambda w: pl.BlockSpec((step, w), lambda i: ((i + 2) % 4, 0))
    whole = lambda a: pl.BlockSpec(a.shape, lambda i: (0, 0))
    return pl.pallas_call(
        qkv_back_kernel,
        grid=(rows // step,),
        in_specs=[by_rows(2 * HD)]
        + [by_rows(2 * HD)] * 4
        + [by_rows(3 * HD), by_rows(HD), by_rows(HD), whole(q_gain), whole(k_gain), by_rows(d), whole(w_qkv)]
        + [by_rows(d), whole(grad_out), whole(grad_gain_ffn)],
        out_specs=[
            pl.BlockSpec((d, 6 * HD), lambda i: (0, 0)),
            pl.BlockSpec((step, d), lambda i: (jnp.maximum(i - 2, 0), 0)),
            pl.BlockSpec((step, d), lambda i: (jnp.minimum(i, 1), 0)),
            pl.BlockSpec((16, d), lambda i: (0, 0)),
        ],
        out_shape=[
            jax.ShapeDtypeStruct((d, 6 * HD), BF),
            jax.ShapeDtypeStruct((rows // 2, d), BF),
            jax.ShapeDtypeStruct((rows // 2, d), BF),
            jax.ShapeDtypeStruct((16, d), F32),
        ],
        scratch_shapes=[pltpu.VMEM((d, 4 * HD), F32)],
        compiler_params=VMEM,
        cost_estimate=cost(1),
        name="project_back",
    )(dq, *dkv, pre, cos, sin, q_gain, k_gain, tokens, w_qkv, norm, grad_out, grad_gain_ffn)


def stacked(ref, i):
    rows = ref[pl.ds(pl.multiple_of(i * BLK, BLK), BLK), :]
    return jnp.concatenate([rows[:, :HD], rows[:, HD:]], axis=0)


def allowed_keys(start, place, first, count):
    pos = first + lax.broadcasted_iota(jnp.int32, (count, 2 * BLK), 0)
    return (pos >= start) & (pos <= place)


def query_places(qblk):
    lane = lax.broadcasted_iota(jnp.int32, (1, 2 * BLK), 1)
    return qblk * BLK + (lane & (BLK - 1))


def attend_kernel(kblk, qblk, low, start_ref, q_ref, kv0, kv1, kv2, kv3, out_ref, o_ref, lse_ref, keys, values_t):
    for s, ref in enumerate((kv0, kv1, kv2, kv3)):
        for j in range(8):
            at = pl.multiple_of(kblk[s * 8 + j] * BLK, BLK)
            keys[pl.ds(at, BLK), :] = ref[j * BLK : (j + 1) * BLK, :HD]
            values_t[:, pl.ds(at, BLK)] = ref[j * BLK : (j + 1) * BLK, HD:].T
    chunk = FWD_KEYS // BLK

    def one_block(i, _):
        q = stacked(q_ref, i)
        start = start_ref[i]
        place = query_places(qblk[i])

        def one_chunk(c, carry):
            acc, total = carry
            first = pl.multiple_of(c * FWD_KEYS, FWD_KEYS)
            scores = contract_last(keys[pl.ds(first, FWD_KEYS), :], q)
            ok = allowed_keys(start, place, first, FWD_KEYS)
            weights = jnp.where(ok, jnp.exp2(scores), 0.0)
            total = total + jnp.sum(weights.reshape(-1, 8, 2 * BLK), axis=0)
            acc = acc + dot(values_t[:, pl.ds(first, FWD_KEYS)], weights.astype(BF))
            return acc, total

        acc, total = lax.fori_loop(
            low[i] // chunk,
            qblk[i] // chunk + 1,
            one_chunk,
            (jnp.zeros((HD, 2 * BLK), F32), jnp.zeros((8, 2 * BLK), F32)),
        )
        total = jnp.sum(total, axis=0, keepdims=True)
        o = acc * (1.0 / total)
        o_ref[i] = o
        lse_ref[i] = jnp.log2(total)
        rows = o.T.astype(BF)
        out_ref[pl.ds(pl.multiple_of(i * BLK, BLK), BLK), :] = jnp.concatenate([rows[:BLK], rows[BLK:]], axis=1)
        return 0

    lax.fori_loop(0, ROWS // BLK, one_block, 0)


def attend(kblk, qblk, low, start, q, kv):
    smem = pl.BlockSpec(memory_space=pltpu.SMEM)
    vmem = pl.BlockSpec(memory_space=pltpu.VMEM)
    blocks = ROWS // BLK
    return pl.pallas_call(
        attend_kernel,
        in_specs=[smem] * 3 + [vmem] * 6,
        out_specs=[vmem] * 3,
        out_shape=[
            jax.ShapeDtypeStruct((ROWS, 2 * HD), BF),
            jax.ShapeDtypeStruct((blocks, HD, 2 * BLK), F32),
            jax.ShapeDtypeStruct((blocks, 1, 2 * BLK), F32),
        ],
        scratch_shapes=[pltpu.VMEM((KEYS, HD), BF), pltpu.VMEM((HD, KEYS), BF)],
        compiler_params=VMEM,
        cost_estimate=cost(1),
        name="attend",
    )(kblk, qblk, low, start, q, *kv)


def attend_back_kernel(
    kblk, qblk, low, start_ref, q_ref, do_ref, o_ref, lse_ref, kv0, kv1, kv2, kv3,
    dq_ref, dkv0, dkv1, dkv2, dkv3, keys, keys_t, values, dk, dv,
):
    for s, ref in enumerate((kv0, kv1, kv2, kv3)):
        for j in range(8):
            at = pl.multiple_of(kblk[s * 8 + j] * BLK, BLK)
            key = ref[j * BLK : (j + 1) * BLK, :HD]
            keys[pl.ds(at, BLK), :] = key
            keys_t[:, pl.ds(at, BLK)] = key.T
            values[pl.ds(at, BLK), :] = ref[j * BLK : (j + 1) * BLK, HD:]
    dk[...] = jnp.zeros_like(dk)
    dv[...] = jnp.zeros_like(dv)
    chunk = BWD_KEYS // BLK

    def one_block(i, _):
        q = stacked(q_ref, i)
        do = stacked(do_ref, i)
        delta = jnp.sum(do.astype(F32).T * o_ref[i], axis=0, keepdims=True)
        lse = lse_ref[i]
        start = start_ref[i]
        place = query_places(qblk[i])

        def one_chunk(c, acc):
            first = pl.multiple_of(c * BWD_KEYS, BWD_KEYS)
            here = pl.ds(first, BWD_KEYS)
            scores = contract_last(keys[here, :], q)
            ok = allowed_keys(start, place, first, BWD_KEYS)
            probs = jnp.where(ok, jnp.exp2(scores - lse), 0.0)
            dprobs = contract_last(values[here, :], do)
            dscores = (probs * (dprobs - delta)).astype(BF)
            dv[here, :] += dot(probs.astype(BF), do)
            dk[here, :] += dot(dscores, q)
            return acc + dot(keys_t[:, here], dscores)

        acc = lax.fori_loop(low[i] // chunk, qblk[i] // chunk + 1, one_chunk, jnp.zeros((HD, 2 * BLK), F32))
        rows = acc.T * SCALE
        dq_ref[pl.ds(pl.multiple_of(i * BLK, BLK), BLK), :] = jnp.concatenate([rows[:BLK], rows[BLK:]], axis=1)
        return 0

    lax.fori_loop(0, ROWS // BLK, one_block, 0)
    for s, ref in enumerate((dkv0, dkv1, dkv2, dkv3)):
        for j in range(8):
            at = pl.multiple_of(kblk[s * 8 + j] * BLK, BLK)
            ref[j * BLK : (j + 1) * BLK, :HD] = (dk[pl.ds(at, BLK), :] * LN2).astype(BF)
            ref[j * BLK : (j + 1) * BLK, HD:] = dv[pl.ds(at, BLK), :].astype(BF)


def attend_back(kblk, qblk, low, start, q, do, o, lse, kv):
    smem = pl.BlockSpec(memory_space=pltpu.SMEM)
    vmem = pl.BlockSpec(memory_space=pltpu.VMEM)
    return pl.pallas_call(
        attend_back_kernel,
        in_specs=[smem] * 3 + [vmem] * 9,
        out_specs=[vmem] * 5,
        out_shape=[jax.ShapeDtypeStruct((ROWS, 2 * HD), F32)] + [jax.ShapeDtypeStruct((ROWS, 2 * HD), BF)] * 4,
        scratch_shapes=[
            pltpu.VMEM((KEYS, HD), BF),
            pltpu.VMEM((HD, KEYS), BF),
            pltpu.VMEM((KEYS, HD), BF),
            pltpu.VMEM((KEYS, HD), F32),
            pltpu.VMEM((KEYS, HD), F32),
        ],
        compiler_params=VMEM,
        cost_estimate=cost(20),
        name="attend_back",
    )(kblk, qblk, low, start, q, do, o, lse, *kv)


def per_device(
    tokens,
    block_table,
    doc_ids,
    attn_gain,
    w_query,
    w_key,
    w_value,
    query_gain,
    key_gain,
    w_out,
    ffn_gain,
    w_gate,
    w_up,
    w_down,
    out_grad,
):
    ctx_rank = lax.axis_index("ctx")
    tp_rank = lax.axis_index("tp")
    x_lo, z, core = ctx_rank // 8, (ctx_rank // 2) % 4, ctx_rank % 2
    y, x_hi = tp_rank // 2, tp_rank % 2
    x = 2 * x_hi + x_lo
    d_model = tokens.shape[1]
    q_width, k_width, ff_local = w_query.shape[1], w_key.shape[1], w_gate.shape[1]

    ring = jnp.array(RING, jnp.int32)
    xs = ((x + ring) % 4)[None, None, :]
    zs = ((z + ring) % 4)[:, None, None]
    cores = ((core + jnp.arange(2, dtype=jnp.int32)) % 2)[None, :, None]
    entry = ((((xs % 2) * 4 + zs) * 2 + cores) * 2 + xs // 2).reshape(32)
    table = block_table.reshape(32)
    kblk = jnp.sum(
        jnp.where(entry[:, None] == jnp.arange(32, dtype=jnp.int32)[None, :], table[None, :], 0), axis=1
    ).astype(jnp.int32)
    qblk = kblk[:8]
    docs = lax.dynamic_index_in_dim(doc_ids, y, 0, keepdims=False)
    firsts = jnp.sum((docs[None, :] < jnp.arange(4, dtype=jnp.int32)[:, None]).astype(jnp.int32), axis=1)
    place = qblk[:, None] * BLK + jnp.arange(BLK, dtype=jnp.int32)[None, :]
    start = jnp.max(
        jnp.where(firsts[:, None, None] <= place[None], firsts[:, None, None], 0), axis=0
    )
    low = start[:, 0] // BLK
    start2 = jnp.concatenate([start, start], axis=1)[:, None, :]
    pos = (place - start).reshape(ROWS)
    freq = jnp.power(jnp.float32(THETA), -(jnp.arange(HD // 2, dtype=F32) * (2.0 / HD)))
    angles = pos.astype(F32)[:, None] * freq[None, :]
    cos_half, sin_half = jnp.cos(angles), jnp.sin(angles)
    cos = jnp.concatenate([cos_half, cos_half], axis=1)
    sin = jnp.concatenate([-sin_half, sin_half], axis=1)
    bits = ((y - jnp.arange(4, dtype=jnp.int32)) % 4)[None, :]
    offs = (((bits // 2) * 4 + zs.reshape(4, 1)) * 2 + bits % 2).reshape(16) * 64

    def head_gain(gain):
        return jnp.concatenate([gain, jnp.zeros((64 - gain.shape[0],), BF)])

    gains = jnp.stack([attn_gain, ffn_gain, head_gain(query_gain), head_gain(key_gain)], axis=1)
    gains = jnp.concatenate([gains, jnp.zeros((64, 124), BF)], axis=1)
    w_o, w_d = w_out.shape[0], w_down.shape[0]
    first_shard = jnp.concatenate([w_query, w_key, w_value, gains, w_out.T], axis=1)
    first_mine = jnp.concatenate(to_users(first_shard), axis=0)
    first = along_z(first_mine)
    w_qkv, gain_cols, w_proj = assembled(first, (q_width + 2 * k_width, 128, w_o), offs)
    gain_rows = gain_cols[:, :8].astype(F32).T
    gain_attn, gain_ffn = gain_rows[0:1], gain_rows[1:2]
    gain_query = gain_rows[2].reshape(16, 64)[:, :8].reshape(1, HD)
    gain_key = gain_rows[3].reshape(16, 64)[:, :8].reshape(1, HD)

    size = tokens.shape[0]
    rows_tok = gather_rows(after(tokens, first_shard))
    normal_one, q, kv, pre = project(rows_tok, gain_attn, w_qkv, gain_query, gain_key, cos, sin)
    kv_all = along_z(kv)
    own_grad, second = after((out_grad, jnp.concatenate([w_gate, w_up, w_down.T], axis=1)), kv)
    half_grad = jnp.concatenate([own_grad] + [shift(own_grad, dx=-d) for d in RING[1:]], axis=0)
    second = to_users(second)
    attn_low, o, lse = attend(kblk, qblk, low, start2, q, kv_all)
    attn_low, second, half_grad = lax.optimization_barrier((attn_low, second, half_grad))
    grad_rows = jnp.concatenate([half_grad, shift(half_grad, dcore=1)], axis=0)
    ffn_slots = along_z(jnp.concatenate(second, axis=0))
    both = sum_product(contract_last, attn_low, w_proj)
    resid = tokens.astype(F32) + summed(both, to_chips(both))
    rate_two = lax.rsqrt(jnp.mean(resid * resid, axis=-1, keepdims=True) + EPS)
    xhat_two = resid * rate_two
    rows_two = gather_rows(after((xhat_two * gain_ffn).astype(BF), ffn_slots[3]), gate=ffn_slots[1:3])
    w_gu, w_dn = assembled(ffn_slots, (2 * ff_local, w_d), offs)
    gate_up = dot(rows_two, w_gu)
    gate, up_proj = gate_up[:, :ff_local], gate_up[:, ff_local:]
    sigmoid_gate = jax.nn.sigmoid(gate)
    silu_gate = gate * sigmoid_gate
    hidden = (silu_gate * up_proj).astype(BF)
    grad_hidden = dot(grad_rows, w_dn)
    grad_gate = grad_hidden * up_proj * (sigmoid_gate * (1.0 + gate * (1.0 - sigmoid_gate)))
    grad_up = grad_hidden * silu_gate
    grad_gu = jnp.concatenate([grad_gate, grad_up], axis=1).astype(BF)
    both = sum_product(contract_last, grad_gu, w_gu)
    rows_now, grads_now, gu_now, hidden_now = after((rows_two, grad_rows, grad_gu, hidden), both)
    ffn_grads = jnp.concatenate([contract_first(rows_now, gu_now), contract_first(grads_now, hidden_now)], axis=1)
    ffn_parts = send_along_z(ffn_grads, z)
    both_out = sum_product(contract_last, hidden_now, w_dn)
    grad_norm_two = summed(both, to_chips(both))
    grad_gain_ffn = jnp.sum(grad_norm_two * xhat_two, axis=0)
    gained = grad_norm_two * gain_ffn
    grad_resid = out_grad.astype(F32) + (
        gained - xhat_two * jnp.mean(gained * xhat_two, axis=-1, keepdims=True)
    ) * rate_two
    branch_rows = gather_rows(after(grad_resid.astype(BF), ffn_parts[1]))
    grad_attn = dot(branch_rows, w_proj).astype(BF)
    grad_attn = after(grad_attn, both_out)
    grad_out = contract_first(branch_rows, attn_low).astype(BF)

    dq, *dkv = attend_back(kblk, qblk, low, start2, q, grad_attn, o, lse, kv_all)
    dkv, ffn_parts[0], both_out = lax.optimization_barrier((dkv, ffn_parts[0], both_out))
    ffn_low = sum_along_z(ffn_parts)
    dkv_all = [dkv[0]] + [shift(dkv[k], dz=RING[k]) for k in range(1, 4)]
    out = (resid + summed(both_out, to_chips(both_out))).astype(BF)
    ffn_owned = to_owners(after(ffn_low, dkv_all[1]), y)
    last_grads, mine, other, sums = project_back(
        dq, dkv_all, pre, cos, sin, gain_query, gain_key, rows_tok, w_qkv, normal_one, grad_out, grad_gain_ffn[None, :]
    )
    last_grads, mine, other, sums, out, ffn_owned = lax.optimization_barrier(
        (last_grads, mine, other, sums, out, ffn_owned)
    )
    last_parts = send_along_z(last_grads, z)
    other, sums = after((other, sums), last_grads)
    sums = (sums + shift(sums, dcore=1)).astype(BF)
    both = sum_cores(other, lambda got: mine.astype(F32) + got).reshape(4, size, d_model)
    both = jnp.concatenate([both, jnp.broadcast_to(sums[None], (4, 16, d_model))], axis=1).reshape(-1, d_model)
    one_parts = to_chips(both)
    grad_norm_one = summed(both, one_parts)
    grad_norm_one, sums = grad_norm_one[:size], grad_norm_one[size:]
    tok = tokens.astype(F32)
    rate_one = lax.rsqrt(jnp.mean(tok * tok, axis=-1, keepdims=True) + EPS)
    xhat_one = tok * rate_one
    gained = grad_norm_one * gain_attn
    grad_x = (
        grad_resid + (gained - xhat_one * jnp.mean(gained * xhat_one, axis=-1, keepdims=True)) * rate_one
    ).astype(BF)
    share, h_share = d_model // 16, HD // 16
    width = 2 * (share + h_share)
    shares = jnp.concatenate(
        [
            sums[0].reshape(16, share),
            sums[1].reshape(16, share),
            sums[2, :HD].reshape(16, h_share),
            sums[3, :HD].reshape(16, h_share),
            jnp.zeros((16, 256 - width), F32),
        ],
        axis=1,
    )
    shares = sum_along_z(send_along_z(shares.astype(BF), z))
    shares = jnp.pad(shares, ((0, 0), (0, 7), (0, last_grads.shape[1] - 256)))
    last_low = sum_along_z(last_parts)
    last_owned = to_owners(jnp.concatenate([last_low, shares], axis=1), y)
    sums = last_owned[share]
    last_owned = last_owned[:share]
    w_all = q_width + 2 * k_width
    return (
        out,
        grad_x,
        sums[:share],
        last_owned[:, :q_width],
        last_owned[:, q_width : q_width + k_width],
        last_owned[:, q_width + k_width : w_all],
        sums[2 * share : 2 * share + h_share],
        sums[2 * share + h_share : width],
        last_owned[:, w_all:].T,
        sums[share : 2 * share],
        ffn_owned[:, :ff_local],
        ffn_owned[:, ff_local : 2 * ff_local],
        ffn_owned[:, 2 * ff_local :].T,
    )


def solution(mesh):
    in_specs = (
        P(("ctx", "tp"), None),
        P(),
        P(),
        P("ctx"),
        P("ctx", "tp"),
        P("ctx", "tp"),
        P("ctx", "tp"),
        P("ctx"),
        P("ctx"),
        P("tp", "ctx"),
        P("ctx"),
        P("ctx", "tp"),
        P("ctx", "tp"),
        P("tp", "ctx"),
        P(("ctx", "tp"), None),
    )
    out_specs = (
        P(("ctx", "tp"), None),
        P(("ctx", "tp"), None),
        P("ctx"),
        P("ctx", "tp"),
        P("ctx", "tp"),
        P("ctx", "tp"),
        P("ctx"),
        P("ctx"),
        P("tp", "ctx"),
        P("ctx"),
        P("ctx", "tp"),
        P("ctx", "tp"),
        P("tp", "ctx"),
    )
    return jax.shard_map(
        per_device, mesh=mesh, in_specs=in_specs, out_specs=out_specs, check_vma=False
    )
```

```python
import functools
import math

import jax
import jax.numpy as jnp
from jax import lax
from jax.experimental import pallas as pl
from jax.experimental.pallas import tpu as pltpu
from jax.sharding import PartitionSpec as P

HD = 128
BLK = 128
EPS = 1e-06
THETA = 1000000.0
SCALE = HD ** (-0.5)
LOG2E = math.log2(math.e)
LN2 = math.log(2.0)
BF = jnp.bfloat16
F32 = jnp.float32
ALL = ("ctx", "tp")
RING = (0, 1, 3, 2)
ROWS = 1024
KEYS = 4096
FWD_KEYS = 1024
BWD_KEYS = 1024
VMEM = pltpu.CompilerParams(vmem_limit_bytes=48 * 1024 * 1024)


def cost(us):
    return pl.CostEstimate(flops=int(us * 1e9), bytes_accessed=int(us * 1e6), transcendentals=0)


def place_of(x, y, z, core):
    x, y, z, core = x % 4, y % 4, z % 4, core % 2
    return (((x % 2) * 4 + z) * 2 + core) * 8 + y * 2 + x // 2


def all_places():
    return [(x, y, z, c) for x in range(4) for y in range(4) for z in range(4) for c in range(2)]


def shift(value, dx=0, dy=0, dz=0, dcore=0):
    pairs = [
        (place_of(x, y, z, c), place_of(x + dx, y + dy, z + dz, c + dcore)) for x, y, z, c in all_places()
    ]
    return lax.ppermute(value, ALL, pairs)


def weight_pairs(step):
    pairs = []
    for x, y, z, c in all_places():
        pairs.append(
            (place_of(x, y, z, c), place_of((x // 2) * 2 + y // 2, (2 * (x % 2) + c + step) % 4, z, y % 2))
        )
    return pairs


def contract_last(left_side, right_side):
    return lax.dot_general(left_side, right_side, (((1,), (1,)), ((), ())), preferred_element_type=F32)


def contract_first(left_side, right_side):
    return lax.dot_general(left_side, right_side, (((0,), (0,)), ((), ())), preferred_element_type=F32)


def dot(left_side, right_side):
    return jnp.dot(left_side, right_side, preferred_element_type=F32)


def gather_rows(own, gate=()):
    half = jnp.concatenate([own] + [shift(own, dx=-d) for d in RING[1:]], axis=0)
    half = after(half, *gate)
    return jnp.concatenate([half, shift(half, dcore=1)], axis=0)


def sum_cores(other, mine):
    got = shift(other, dcore=1)
    return mine(got.astype(F32)).astype(BF)


def to_chips(both):
    rows = both.shape[0] // 4
    return [shift(both[k * rows : (k + 1) * rows], dx=RING[k]) for k in range(1, 4)]


def summed(both, arrived):
    total = both[: both.shape[0] // 4].astype(F32)
    for part in arrived:
        total = total + part.astype(F32)
    return total


def sum_product(product, left_side, right_side):
    half = left_side.shape[0] // 2
    other = product(left_side[half:], right_side).astype(BF)
    return sum_cores(other, lambda got: product(left_side[:half], right_side) + got)


def after(values, *others):
    return lax.optimization_barrier((values, others))[0]


def assemble_kernel(widths, offs_ref, *refs):
    slots, outs = refs[:4], refs[4:]
    for s in range(4):
        for k in range(4):
            rows = pl.ds(pl.multiple_of(offs_ref[s * 4 + k], 64), 64)
            col = 0
            for out, width in zip(outs, widths, strict=True):
                out[rows, :] = slots[s][k * 64 : (k + 1) * 64, col : col + width]
                col += width


def to_users(shard):
    return [lax.ppermute(shard, ALL, weight_pairs(step)) for step in range(4)]


def along_z(mine):
    return [mine] + [shift(mine, dz=-d) for d in RING[1:]]


def assembled(slots, widths, offs):
    vmem = pl.BlockSpec(memory_space=pltpu.VMEM)
    return pl.pallas_call(
        functools.partial(assemble_kernel, widths),
        out_shape=[jax.ShapeDtypeStruct((ROWS, w), BF) for w in widths],
        in_specs=[pl.BlockSpec(memory_space=pltpu.SMEM)] + [vmem] * 4,
        out_specs=[vmem] * len(widths),
        compiler_params=VMEM,
        cost_estimate=cost(1 + sum(widths) / 512),
        name="assemble",
    )(offs, *slots)


def send_along_z(grads, z):
    parts = grads.astype(BF).reshape(2, 4, 2, -1, grads.shape[-1])

    def rows_for(d):
        return lax.dynamic_index_in_dim(parts, (z + d) % 4, 1, keepdims=False)

    return [rows_for(0)] + [shift(rows_for(d), dz=d) for d in RING[1:]]


def sum_along_z(parts):
    total = parts[0].astype(F32)
    for part in parts[1:]:
        total = total + part.astype(F32)
    return total.astype(BF).reshape(4, -1, parts[0].shape[-1])


def to_owners(low, y):
    result = None
    for step in range(4):
        piece = lax.dynamic_index_in_dim(low, (y - step) % 4, 0, keepdims=False)
        back = [(b, a) for a, b in weight_pairs(step)]
        got = lax.ppermute(piece, ALL, back).astype(F32)
        result = got if result is None else result + got
    return result


def head_norm(pre):
    return pre * lax.rsqrt(jnp.mean(pre * pre, axis=-1, keepdims=True) + EPS)


def qkv_kernel(tok_ref, gain_ref, w_ref, qg_ref, kg_ref, cos_ref, sin_ref, norm_ref, q_ref, kv_ref, pre_ref):
    tok = tok_ref[...].astype(F32)
    rate = lax.rsqrt(jnp.mean(tok * tok, axis=-1, keepdims=True) + EPS)
    low = (tok * rate * gain_ref[...]).astype(BF)
    norm_ref[...] = low
    proj = dot(low, w_ref[...])
    cos, sin = cos_ref[...], sin_ref[...]
    pre_ref[...] = proj[:, : 3 * HD]
    for h in range(3):
        gain = qg_ref[...] if h < 2 else kg_ref[...]
        u = head_norm(proj[:, h * HD : (h + 1) * HD]) * gain
        u = u * cos + pltpu.roll(u, HD // 2, 1) * sin
        if h < 2:
            q_ref[:, h * HD : (h + 1) * HD] = (u * (SCALE * LOG2E)).astype(BF)
        else:
            kv_ref[:, :HD] = u.astype(BF)
    kv_ref[:, HD:] = proj[:, 3 * HD :].astype(BF)


def project(tokens, gain, w_qkv, q_gain, k_gain, cos, sin):
    rows, d = tokens.shape
    step = 256
    by_rows = lambda w: pl.BlockSpec((step, w), lambda i: (i, 0))
    whole = lambda a: pl.BlockSpec(a.shape, lambda i: (0, 0))
    return pl.pallas_call(
        qkv_kernel,
        grid=(rows // step,),
        in_specs=[by_rows(d), whole(gain), whole(w_qkv), whole(q_gain), whole(k_gain), by_rows(HD), by_rows(HD)],
        out_specs=[by_rows(d), by_rows(2 * HD), by_rows(2 * HD), by_rows(3 * HD)],
        out_shape=[
            jax.ShapeDtypeStruct((rows, d), BF),
            jax.ShapeDtypeStruct((rows, 2 * HD), BF),
            jax.ShapeDtypeStruct((rows, 2 * HD), BF),
            jax.ShapeDtypeStruct((rows, 3 * HD), F32),
        ],
        compiler_params=VMEM,
        cost_estimate=cost(1),
        name="project",
    )(tokens, gain, w_qkv, q_gain, k_gain, cos, sin)


def qkv_back_kernel(
    dq_ref, kv0, kv1, kv2, kv3, pre_ref, cos_ref, sin_ref, qg_ref, kg_ref, tok_ref, w_ref, norm_ref, gout_ref, gffn_ref,
    gw_ref, mine_ref, other_ref, sums_ref, gw_sum,
):
    step = pl.program_id(0)

    @pl.when(step == 0)
    def _():
        sums_ref[...] = jnp.zeros_like(sums_ref)
        sums_ref[1:2, :] = gffn_ref[...]
        gw_sum[...] = jnp.zeros_like(gw_sum)

    dkv = kv0[...].astype(F32) + kv1[...].astype(F32) + kv2[...].astype(F32) + kv3[...].astype(F32)
    cos, sin = cos_ref[...], sin_ref[...]
    grads = []
    for h in range(3):
        grad = dq_ref[:, h * HD : (h + 1) * HD] if h < 2 else dkv[:, :HD]
        gain = qg_ref[...] if h < 2 else kg_ref[...]
        u = pre_ref[:, h * HD : (h + 1) * HD]
        rate = lax.rsqrt(jnp.mean(u * u, axis=-1, keepdims=True) + EPS)
        n = u * rate
        g = grad * cos - pltpu.roll(grad, HD // 2, 1) * sin
        gained = gain * g
        pre_grad = (gained - n * jnp.mean(gained * n, axis=-1, keepdims=True)) * rate
        grads.append(pre_grad.astype(BF))
        row = 2 if h < 2 else 3
        sums_ref[row : row + 1, :HD] += jnp.sum(g * n, axis=0, keepdims=True)
    gqkv = jnp.concatenate(grads + [dkv[:, HD:].astype(BF)], axis=1)
    gw_sum[...] += contract_first(norm_ref[...], gqkv)
    gnorm = contract_last(gqkv, w_ref[...])

    @pl.when(step < 2)
    def _():
        other_ref[...] = gnorm.astype(BF)

    @pl.when(step >= 2)
    def _():
        mine_ref[...] = gnorm.astype(BF)

    tok = tok_ref[...].astype(F32)
    xhat = tok * lax.rsqrt(jnp.mean(tok * tok, axis=-1, keepdims=True) + EPS)
    sums_ref[0:1, :] += jnp.sum(gnorm * xhat, axis=0, keepdims=True)

    @pl.when(step == 3)
    def _():
        gw_ref[:, : 4 * HD] = gw_sum[...].astype(BF)
        gw_ref[:, 4 * HD :] = gout_ref[...]


def project_back(dq, dkv, pre, cos, sin, q_gain, k_gain, tokens, w_qkv, norm, grad_out, grad_gain_ffn):
    rows, d = tokens.shape
    step = 256
    by_rows = lambda w: pl.BlockSpec((step, w), lambda i: ((i + 2) % 4, 0))
    whole = lambda a: pl.BlockSpec(a.shape, lambda i: (0, 0))
    return pl.pallas_call(
        qkv_back_kernel,
        grid=(rows // step,),
        in_specs=[by_rows(2 * HD)]
        + [by_rows(2 * HD)] * 4
        + [by_rows(3 * HD), by_rows(HD), by_rows(HD), whole(q_gain), whole(k_gain), by_rows(d), whole(w_qkv)]
        + [by_rows(d), whole(grad_out), whole(grad_gain_ffn)],
        out_specs=[
            pl.BlockSpec((d, 6 * HD), lambda i: (0, 0)),
            pl.BlockSpec((step, d), lambda i: (jnp.maximum(i - 2, 0), 0)),
            pl.BlockSpec((step, d), lambda i: (jnp.minimum(i, 1), 0)),
            pl.BlockSpec((16, d), lambda i: (0, 0)),
        ],
        out_shape=[
            jax.ShapeDtypeStruct((d, 6 * HD), BF),
            jax.ShapeDtypeStruct((rows // 2, d), BF),
            jax.ShapeDtypeStruct((rows // 2, d), BF),
            jax.ShapeDtypeStruct((16, d), F32),
        ],
        scratch_shapes=[pltpu.VMEM((d, 4 * HD), F32)],
        compiler_params=VMEM,
        cost_estimate=cost(1),
        name="project_back",
    )(dq, *dkv, pre, cos, sin, q_gain, k_gain, tokens, w_qkv, norm, grad_out, grad_gain_ffn)


def stacked(ref, i):
    rows = ref[pl.ds(pl.multiple_of(i * BLK, BLK), BLK), :]
    return jnp.concatenate([rows[:, :HD], rows[:, HD:]], axis=0)


def allowed_keys(start, place, first, count):
    pos = first + lax.broadcasted_iota(jnp.int32, (count, 2 * BLK), 0)
    return (pos >= start) & (pos <= place)


def query_places(qblk):
    lane = lax.broadcasted_iota(jnp.int32, (1, 2 * BLK), 1)
    return qblk * BLK + (lane & (BLK - 1))


def attend_kernel(kblk, qblk, low, start_ref, q_ref, kv0, kv1, kv2, kv3, out_ref, o_ref, lse_ref, keys, values_t):
    for s, ref in enumerate((kv0, kv1, kv2, kv3)):
        for j in range(8):
            at = pl.multiple_of(kblk[s * 8 + j] * BLK, BLK)
            keys[pl.ds(at, BLK), :] = ref[j * BLK : (j + 1) * BLK, :HD]
            values_t[:, pl.ds(at, BLK)] = ref[j * BLK : (j + 1) * BLK, HD:].T
    keys[KEYS:, :] = jnp.zeros((FWD_KEYS, HD), BF)
    values_t[:, KEYS:] = jnp.zeros((HD, FWD_KEYS), BF)

    def one_block(i, _):
        q = stacked(q_ref, i)
        start = start_ref[i]
        place = query_places(qblk[i])

        def one_chunk(c, carry):
            acc, total = carry
            first = pl.multiple_of((low[i] + c * (FWD_KEYS // BLK)) * BLK, BLK)
            scores = contract_last(keys[pl.ds(first, FWD_KEYS), :], q)
            ok = allowed_keys(start, place, first, FWD_KEYS)
            weights = jnp.where(ok, jnp.exp2(scores), 0.0)
            total = total + jnp.sum(weights.reshape(-1, 8, 2 * BLK), axis=0)
            acc = acc + dot(values_t[:, pl.ds(first, FWD_KEYS)], weights.astype(BF))
            return acc, total

        acc, total = lax.fori_loop(
            0,
            (qblk[i] - low[i]) // (FWD_KEYS // BLK) + 1,
            one_chunk,
            (jnp.zeros((HD, 2 * BLK), F32), jnp.zeros((8, 2 * BLK), F32)),
        )
        total = jnp.sum(total, axis=0, keepdims=True)
        o = acc * (1.0 / total)
        o_ref[i] = o
        lse_ref[i] = jnp.log2(total)
        rows = o.T.astype(BF)
        out_ref[pl.ds(pl.multiple_of(i * BLK, BLK), BLK), :] = jnp.concatenate([rows[:BLK], rows[BLK:]], axis=1)
        return 0

    lax.fori_loop(0, ROWS // BLK, one_block, 0)


def attend(kblk, qblk, low, start, q, kv):
    smem = pl.BlockSpec(memory_space=pltpu.SMEM)
    vmem = pl.BlockSpec(memory_space=pltpu.VMEM)
    blocks = ROWS // BLK
    return pl.pallas_call(
        attend_kernel,
        in_specs=[smem] * 3 + [vmem] * 6,
        out_specs=[vmem] * 3,
        out_shape=[
            jax.ShapeDtypeStruct((ROWS, 2 * HD), BF),
            jax.ShapeDtypeStruct((blocks, HD, 2 * BLK), F32),
            jax.ShapeDtypeStruct((blocks, 1, 2 * BLK), F32),
        ],
        scratch_shapes=[pltpu.VMEM((KEYS + FWD_KEYS, HD), BF), pltpu.VMEM((HD, KEYS + FWD_KEYS), BF)],
        compiler_params=VMEM,
        cost_estimate=cost(1),
        name="attend",
    )(kblk, qblk, low, start, q, *kv)


def attend_back_kernel(
    kblk, qblk, low, start_ref, q_ref, do_ref, o_ref, lse_ref, kv0, kv1, kv2, kv3,
    dq_ref, dkv0, dkv1, dkv2, dkv3, keys, keys_t, values, dk, dv,
):
    for s, ref in enumerate((kv0, kv1, kv2, kv3)):
        for j in range(8):
            at = pl.multiple_of(kblk[s * 8 + j] * BLK, BLK)
            key = ref[j * BLK : (j + 1) * BLK, :HD]
            keys[pl.ds(at, BLK), :] = key
            keys_t[:, pl.ds(at, BLK)] = key.T
            values[pl.ds(at, BLK), :] = ref[j * BLK : (j + 1) * BLK, HD:]
    dk[...] = jnp.zeros_like(dk)
    dv[...] = jnp.zeros_like(dv)
    keys[KEYS:, :] = jnp.zeros((BWD_KEYS, HD), BF)
    keys_t[:, KEYS:] = jnp.zeros((HD, BWD_KEYS), BF)
    values[KEYS:, :] = jnp.zeros((BWD_KEYS, HD), BF)

    def one_block(i, _):
        q = stacked(q_ref, i)
        do = stacked(do_ref, i)
        delta = jnp.sum(do.astype(F32).T * o_ref[i], axis=0, keepdims=True)
        lse = lse_ref[i]
        start = start_ref[i]
        place = query_places(qblk[i])

        def one_chunk(c, acc):
            first = pl.multiple_of((low[i] + c * (BWD_KEYS // BLK)) * BLK, BLK)
            here = pl.ds(first, BWD_KEYS)
            scores = contract_last(keys[here, :], q)
            ok = allowed_keys(start, place, first, BWD_KEYS)
            probs = jnp.where(ok, jnp.exp2(scores - lse), 0.0)
            dprobs = contract_last(values[here, :], do)
            dscores = (probs * (dprobs - delta)).astype(BF)
            dv[here, :] += dot(probs.astype(BF), do)
            dk[here, :] += dot(dscores, q)
            return acc + dot(keys_t[:, here], dscores)

        acc = lax.fori_loop(0, (qblk[i] - low[i]) // (BWD_KEYS // BLK) + 1, one_chunk, jnp.zeros((HD, 2 * BLK), F32))
        rows = acc.T * SCALE
        dq_ref[pl.ds(pl.multiple_of(i * BLK, BLK), BLK), :] = jnp.concatenate([rows[:BLK], rows[BLK:]], axis=1)
        return 0

    lax.fori_loop(0, ROWS // BLK, one_block, 0)
    for s, ref in enumerate((dkv0, dkv1, dkv2, dkv3)):
        for j in range(8):
            at = pl.multiple_of(kblk[s * 8 + j] * BLK, BLK)
            ref[j * BLK : (j + 1) * BLK, :HD] = (dk[pl.ds(at, BLK), :] * LN2).astype(BF)
            ref[j * BLK : (j + 1) * BLK, HD:] = dv[pl.ds(at, BLK), :].astype(BF)


def attend_back(kblk, qblk, low, start, q, do, o, lse, kv):
    smem = pl.BlockSpec(memory_space=pltpu.SMEM)
    vmem = pl.BlockSpec(memory_space=pltpu.VMEM)
    return pl.pallas_call(
        attend_back_kernel,
        in_specs=[smem] * 3 + [vmem] * 9,
        out_specs=[vmem] * 5,
        out_shape=[jax.ShapeDtypeStruct((ROWS, 2 * HD), F32)] + [jax.ShapeDtypeStruct((ROWS, 2 * HD), BF)] * 4,
        scratch_shapes=[
            pltpu.VMEM((KEYS + BWD_KEYS, HD), BF),
            pltpu.VMEM((HD, KEYS + BWD_KEYS), BF),
            pltpu.VMEM((KEYS + BWD_KEYS, HD), BF),
            pltpu.VMEM((KEYS + BWD_KEYS, HD), F32),
            pltpu.VMEM((KEYS + BWD_KEYS, HD), F32),
        ],
        compiler_params=VMEM,
        cost_estimate=cost(20),
        name="attend_back",
    )(kblk, qblk, low, start, q, do, o, lse, *kv)


def per_device(
    tokens,
    block_table,
    doc_ids,
    attn_gain,
    w_query,
    w_key,
    w_value,
    query_gain,
    key_gain,
    w_out,
    ffn_gain,
    w_gate,
    w_up,
    w_down,
    out_grad,
):
    ctx_rank = lax.axis_index("ctx")
    tp_rank = lax.axis_index("tp")
    x_lo, z, core = ctx_rank // 8, (ctx_rank // 2) % 4, ctx_rank % 2
    y, x_hi = tp_rank // 2, tp_rank % 2
    x = 2 * x_hi + x_lo
    d_model = tokens.shape[1]
    q_width, k_width, ff_local = w_query.shape[1], w_key.shape[1], w_gate.shape[1]

    ring = jnp.array(RING, jnp.int32)
    xs = ((x + ring) % 4)[None, None, :]
    zs = ((z + ring) % 4)[:, None, None]
    cores = ((core + jnp.arange(2, dtype=jnp.int32)) % 2)[None, :, None]
    entry = ((((xs % 2) * 4 + zs) * 2 + cores) * 2 + xs // 2).reshape(32)
    table = block_table.reshape(32)
    kblk = jnp.sum(
        jnp.where(entry[:, None] == jnp.arange(32, dtype=jnp.int32)[None, :], table[None, :], 0), axis=1
    ).astype(jnp.int32)
    qblk = kblk[:8]
    docs = lax.dynamic_index_in_dim(doc_ids, y, 0, keepdims=False)
    firsts = jnp.sum((docs[None, :] < jnp.arange(4, dtype=jnp.int32)[:, None]).astype(jnp.int32), axis=1)
    place = qblk[:, None] * BLK + jnp.arange(BLK, dtype=jnp.int32)[None, :]
    start = jnp.max(
        jnp.where(firsts[:, None, None] <= place[None], firsts[:, None, None], 0), axis=0
    )
    low = start[:, 0] // BLK
    start2 = jnp.concatenate([start, start], axis=1)[:, None, :]
    pos = (place - start).reshape(ROWS)
    freq = jnp.power(jnp.float32(THETA), -(jnp.arange(HD // 2, dtype=F32) * (2.0 / HD)))
    angles = pos.astype(F32)[:, None] * freq[None, :]
    cos_half, sin_half = jnp.cos(angles), jnp.sin(angles)
    cos = jnp.concatenate([cos_half, cos_half], axis=1)
    sin = jnp.concatenate([-sin_half, sin_half], axis=1)
    bits = ((y - jnp.arange(4, dtype=jnp.int32)) % 4)[None, :]
    offs = (((bits // 2) * 4 + zs.reshape(4, 1)) * 2 + bits % 2).reshape(16) * 64

    def head_gain(gain):
        return jnp.concatenate([gain, jnp.zeros((64 - gain.shape[0],), BF)])

    gains = jnp.stack([attn_gain, ffn_gain, head_gain(query_gain), head_gain(key_gain)], axis=1)
    gains = jnp.concatenate([gains, jnp.zeros((64, 124), BF)], axis=1)
    w_o, w_d = w_out.shape[0], w_down.shape[0]
    first_shard = jnp.concatenate([w_query, w_key, w_value, gains, w_out.T], axis=1)
    first_mine = jnp.concatenate(to_users(first_shard), axis=0)
    first = along_z(first_mine)
    w_qkv, gain_cols, w_proj = assembled(first, (q_width + 2 * k_width, 128, w_o), offs)
    gain_rows = gain_cols[:, :8].astype(F32).T
    gain_attn, gain_ffn = gain_rows[0:1], gain_rows[1:2]
    gain_query = gain_rows[2].reshape(16, 64)[:, :8].reshape(1, HD)
    gain_key = gain_rows[3].reshape(16, 64)[:, :8].reshape(1, HD)

    size = tokens.shape[0]
    rows_tok = gather_rows(after(tokens, first_shard))
    normal_one, q, kv, pre = project(rows_tok, gain_attn, w_qkv, gain_query, gain_key, cos, sin)
    kv_all = along_z(kv)
    own_grad, second = after((out_grad, jnp.concatenate([w_gate, w_up, w_down.T], axis=1)), kv)
    half_grad = jnp.concatenate([own_grad] + [shift(own_grad, dx=-d) for d in RING[1:]], axis=0)
    second = to_users(second)
    attn_low, o, lse = attend(kblk, qblk, low, start2, q, kv_all)
    attn_low, second, half_grad = lax.optimization_barrier((attn_low, second, half_grad))
    grad_rows = jnp.concatenate([half_grad, shift(half_grad, dcore=1)], axis=0)
    ffn_slots = along_z(jnp.concatenate(second, axis=0))
    both = sum_product(contract_last, attn_low, w_proj)
    resid = tokens.astype(F32) + summed(both, to_chips(both))
    rate_two = lax.rsqrt(jnp.mean(resid * resid, axis=-1, keepdims=True) + EPS)
    xhat_two = resid * rate_two
    rows_two = gather_rows(after((xhat_two * gain_ffn).astype(BF), ffn_slots[3]), gate=ffn_slots[1:3])
    w_gu, w_dn = assembled(ffn_slots, (2 * ff_local, w_d), offs)
    gate_up = dot(rows_two, w_gu)
    gate, up_proj = gate_up[:, :ff_local], gate_up[:, ff_local:]
    sigmoid_gate = jax.nn.sigmoid(gate)
    silu_gate = gate * sigmoid_gate
    hidden = (silu_gate * up_proj).astype(BF)
    grad_hidden = dot(grad_rows, w_dn)
    grad_gate = grad_hidden * up_proj * (sigmoid_gate * (1.0 + gate * (1.0 - sigmoid_gate)))
    grad_up = grad_hidden * silu_gate
    grad_gu = jnp.concatenate([grad_gate, grad_up], axis=1).astype(BF)
    both = sum_product(contract_last, grad_gu, w_gu)
    rows_now, grads_now, gu_now, hidden_now = after((rows_two, grad_rows, grad_gu, hidden), both)
    ffn_grads = jnp.concatenate([contract_first(rows_now, gu_now), contract_first(grads_now, hidden_now)], axis=1)
    ffn_parts = send_along_z(ffn_grads, z)
    both_out = sum_product(contract_last, hidden_now, w_dn)
    grad_norm_two = summed(both, to_chips(both))
    grad_gain_ffn = jnp.sum(grad_norm_two * xhat_two, axis=0)
    gained = grad_norm_two * gain_ffn
    grad_resid = out_grad.astype(F32) + (
        gained - xhat_two * jnp.mean(gained * xhat_two, axis=-1, keepdims=True)
    ) * rate_two
    branch_rows = gather_rows(after(grad_resid.astype(BF), ffn_parts[1]))
    grad_attn = dot(branch_rows, w_proj).astype(BF)
    grad_attn = after(grad_attn, both_out)
    grad_out = contract_first(branch_rows, attn_low).astype(BF)

    dq, *dkv = attend_back(kblk, qblk, low, start2, q, grad_attn, o, lse, kv_all)
    dkv, ffn_parts[0], both_out = lax.optimization_barrier((dkv, ffn_parts[0], both_out))
    ffn_low = sum_along_z(ffn_parts)
    dkv_all = [dkv[0]] + [shift(dkv[k], dz=RING[k]) for k in range(1, 4)]
    out = (resid + summed(both_out, to_chips(both_out))).astype(BF)
    ffn_owned = to_owners(after(ffn_low, dkv_all[1]), y)
    last_grads, mine, other, sums = project_back(
        dq, dkv_all, pre, cos, sin, gain_query, gain_key, rows_tok, w_qkv, normal_one, grad_out, grad_gain_ffn[None, :]
    )
    last_grads, mine, other, sums, out, ffn_owned = lax.optimization_barrier(
        (last_grads, mine, other, sums, out, ffn_owned)
    )
    last_parts = send_along_z(last_grads, z)
    other, sums = after((other, sums), last_grads)
    sums = (sums + shift(sums, dcore=1)).astype(BF)
    both = sum_cores(other, lambda got: mine.astype(F32) + got).reshape(4, size, d_model)
    both = jnp.concatenate([both, jnp.broadcast_to(sums[None], (4, 16, d_model))], axis=1).reshape(-1, d_model)
    one_parts = to_chips(both)
    grad_norm_one = summed(both, one_parts)
    grad_norm_one, sums = grad_norm_one[:size], grad_norm_one[size:]
    tok = tokens.astype(F32)
    rate_one = lax.rsqrt(jnp.mean(tok * tok, axis=-1, keepdims=True) + EPS)
    xhat_one = tok * rate_one
    gained = grad_norm_one * gain_attn
    grad_x = (
        grad_resid + (gained - xhat_one * jnp.mean(gained * xhat_one, axis=-1, keepdims=True)) * rate_one
    ).astype(BF)
    share, h_share = d_model // 16, HD // 16
    width = 2 * (share + h_share)
    shares = jnp.concatenate(
        [
            sums[0].reshape(16, share),
            sums[1].reshape(16, share),
            sums[2, :HD].reshape(16, h_share),
            sums[3, :HD].reshape(16, h_share),
            jnp.zeros((16, 256 - width), F32),
        ],
        axis=1,
    )
    shares = sum_along_z(send_along_z(shares.astype(BF), z))
    shares = jnp.pad(shares, ((0, 0), (0, 7), (0, last_grads.shape[1] - 256)))
    last_low = sum_along_z(after(last_parts, one_parts))
    last_owned = to_owners(jnp.concatenate([last_low, shares], axis=1), y)
    sums = last_owned[share]
    last_owned = last_owned[:share]
    w_all = q_width + 2 * k_width
    return (
        out,
        grad_x,
        sums[:share],
        last_owned[:, :q_width],
        last_owned[:, q_width : q_width + k_width],
        last_owned[:, q_width + k_width : w_all],
        sums[2 * share : 2 * share + h_share],
        sums[2 * share + h_share : width],
        last_owned[:, w_all:].T,
        sums[share : 2 * share],
        ffn_owned[:, :ff_local],
        ffn_owned[:, ff_local : 2 * ff_local],
        ffn_owned[:, 2 * ff_local :].T,
    )


def solution(mesh):
    in_specs = (
        P(("ctx", "tp"), None),
        P(),
        P(),
        P("ctx"),
        P("ctx", "tp"),
        P("ctx", "tp"),
        P("ctx", "tp"),
        P("ctx"),
        P("ctx"),
        P("tp", "ctx"),
        P("ctx"),
        P("ctx", "tp"),
        P("ctx", "tp"),
        P("tp", "ctx"),
        P(("ctx", "tp"), None),
    )
    out_specs = (
        P(("ctx", "tp"), None),
        P(("ctx", "tp"), None),
        P("ctx"),
        P("ctx", "tp"),
        P("ctx", "tp"),
        P("ctx", "tp"),
        P("ctx"),
        P("ctx"),
        P("tp", "ctx"),
        P("ctx"),
        P("ctx", "tp"),
        P("ctx", "tp"),
        P("tp", "ctx"),
    )
    return jax.shard_map(
        per_device, mesh=mesh, in_specs=in_specs, out_specs=out_specs, check_vma=False
    )
```

```python
import functools
import math

import jax
import jax.numpy as jnp
from jax import lax
from jax.experimental import pallas as pl
from jax.experimental.pallas import tpu as pltpu
from jax.sharding import PartitionSpec as P

HD = 128
BLK = 128
EPS = 1e-06
THETA = 1000000.0
SCALE = HD ** (-0.5)
LOG2E = math.log2(math.e)
LN2 = math.log(2.0)
BF = jnp.bfloat16
F32 = jnp.float32
ALL = ("ctx", "tp")
RING = (0, 1, 3, 2)
ROWS = 1024
KEYS = 4096
FWD_KEYS = 1024
BWD_KEYS = 1024
VMEM = pltpu.CompilerParams(vmem_limit_bytes=48 * 1024 * 1024)


def cost(us):
    return pl.CostEstimate(flops=int(us * 1e9), bytes_accessed=int(us * 1e6), transcendentals=0)


def place_of(x, y, z, core):
    x, y, z, core = x % 4, y % 4, z % 4, core % 2
    return (((x % 2) * 4 + z) * 2 + core) * 8 + y * 2 + x // 2


def all_places():
    return [(x, y, z, c) for x in range(4) for y in range(4) for z in range(4) for c in range(2)]


def shift(value, dx=0, dy=0, dz=0, dcore=0):
    pairs = [
        (place_of(x, y, z, c), place_of(x + dx, y + dy, z + dz, c + dcore)) for x, y, z, c in all_places()
    ]
    return lax.ppermute(value, ALL, pairs)


def weight_pairs(step):
    pairs = []
    for x, y, z, c in all_places():
        pairs.append(
            (place_of(x, y, z, c), place_of((x // 2) * 2 + y // 2, (2 * (x % 2) + c + step) % 4, z, y % 2))
        )
    return pairs


def contract_last(left_side, right_side):
    return lax.dot_general(left_side, right_side, (((1,), (1,)), ((), ())), preferred_element_type=F32)


def contract_first(left_side, right_side):
    return lax.dot_general(left_side, right_side, (((0,), (0,)), ((), ())), preferred_element_type=F32)


def dot(left_side, right_side):
    return jnp.dot(left_side, right_side, preferred_element_type=F32)


def gather_rows(own, gate=()):
    half = jnp.concatenate([own] + [shift(own, dx=-d) for d in RING[1:]], axis=0)
    half = after(half, *gate)
    return jnp.concatenate([half, shift(half, dcore=1)], axis=0)


def sum_cores(other, mine):
    got = shift(other, dcore=1)
    return mine(got.astype(F32)).astype(BF)


def to_chips(both):
    rows = both.shape[0] // 4
    return [shift(both[k * rows : (k + 1) * rows], dx=RING[k]) for k in range(1, 4)]


def summed(both, arrived):
    total = both[: both.shape[0] // 4].astype(F32)
    for part in arrived:
        total = total + part.astype(F32)
    return total


def sum_product(product, left_side, right_side):
    half = left_side.shape[0] // 2
    other = product(left_side[half:], right_side).astype(BF)
    return sum_cores(other, lambda got: product(left_side[:half], right_side) + got)


def after(values, *others):
    return lax.optimization_barrier((values, others))[0]


def assemble_kernel(widths, offs_ref, *refs):
    slots, outs = refs[:4], refs[4:]
    for s in range(4):
        for k in range(4):
            rows = pl.ds(pl.multiple_of(offs_ref[s * 4 + k], 64), 64)
            col = 0
            for out, width in zip(outs, widths, strict=True):
                out[rows, :] = slots[s][k * 64 : (k + 1) * 64, col : col + width]
                col += width


def to_users(shard):
    return [lax.ppermute(shard, ALL, weight_pairs(step)) for step in range(4)]


def along_z(mine):
    return [mine] + [shift(mine, dz=-d) for d in RING[1:]]


def assembled(slots, widths, offs):
    vmem = pl.BlockSpec(memory_space=pltpu.VMEM)
    return pl.pallas_call(
        functools.partial(assemble_kernel, widths),
        out_shape=[jax.ShapeDtypeStruct((ROWS, w), BF) for w in widths],
        in_specs=[pl.BlockSpec(memory_space=pltpu.SMEM)] + [vmem] * 4,
        out_specs=[vmem] * len(widths),
        compiler_params=VMEM,
        cost_estimate=cost(1 + sum(widths) / 512),
        name="assemble",
    )(offs, *slots)


def send_along_z(grads, z):
    parts = grads.astype(BF).reshape(2, 4, 2, -1, grads.shape[-1])

    def rows_for(d):
        return lax.dynamic_index_in_dim(parts, (z + d) % 4, 1, keepdims=False)

    return [rows_for(0)] + [shift(rows_for(d), dz=d) for d in RING[1:]]


def sum_along_z(parts):
    total = parts[0].astype(F32)
    for part in parts[1:]:
        total = total + part.astype(F32)
    return total.astype(BF).reshape(4, -1, parts[0].shape[-1])


def to_owners(low, y):
    result = None
    for step in range(4):
        piece = lax.dynamic_index_in_dim(low, (y - step) % 4, 0, keepdims=False)
        back = [(b, a) for a, b in weight_pairs(step)]
        got = lax.ppermute(piece, ALL, back).astype(F32)
        result = got if result is None else result + got
    return result


def head_norm(pre):
    return pre * lax.rsqrt(jnp.mean(pre * pre, axis=-1, keepdims=True) + EPS)


def qkv_kernel(tok_ref, gain_ref, w_ref, qg_ref, kg_ref, cos_ref, sin_ref, norm_ref, q_ref, kv_ref, pre_ref):
    tok = tok_ref[...].astype(F32)
    rate = lax.rsqrt(jnp.mean(tok * tok, axis=-1, keepdims=True) + EPS)
    low = (tok * rate * gain_ref[...]).astype(BF)
    norm_ref[...] = low
    proj = dot(low, w_ref[...])
    cos, sin = cos_ref[...], sin_ref[...]
    pre_ref[...] = proj[:, : 3 * HD]
    for h in range(3):
        gain = qg_ref[...] if h < 2 else kg_ref[...]
        u = head_norm(proj[:, h * HD : (h + 1) * HD]) * gain
        u = u * cos + pltpu.roll(u, HD // 2, 1) * sin
        if h < 2:
            q_ref[:, h * HD : (h + 1) * HD] = (u * (SCALE * LOG2E)).astype(BF)
        else:
            kv_ref[:, :HD] = u.astype(BF)
    kv_ref[:, HD:] = proj[:, 3 * HD :].astype(BF)


def project(tokens, gain, w_qkv, q_gain, k_gain, cos, sin):
    rows, d = tokens.shape
    step = 256
    by_rows = lambda w: pl.BlockSpec((step, w), lambda i: (i, 0))
    whole = lambda a: pl.BlockSpec(a.shape, lambda i: (0, 0))
    return pl.pallas_call(
        qkv_kernel,
        grid=(rows // step,),
        in_specs=[by_rows(d), whole(gain), whole(w_qkv), whole(q_gain), whole(k_gain), by_rows(HD), by_rows(HD)],
        out_specs=[by_rows(d), by_rows(2 * HD), by_rows(2 * HD), by_rows(3 * HD)],
        out_shape=[
            jax.ShapeDtypeStruct((rows, d), BF),
            jax.ShapeDtypeStruct((rows, 2 * HD), BF),
            jax.ShapeDtypeStruct((rows, 2 * HD), BF),
            jax.ShapeDtypeStruct((rows, 3 * HD), F32),
        ],
        compiler_params=VMEM,
        cost_estimate=cost(1),
        name="project",
    )(tokens, gain, w_qkv, q_gain, k_gain, cos, sin)


def qkv_back_kernel(
    dq_ref, kv0, kv1, kv2, kv3, pre_ref, cos_ref, sin_ref, qg_ref, kg_ref, tok_ref, w_ref, norm_ref, gout_ref, gffn_ref,
    gw_ref, mine_ref, other_ref, sums_ref, gw_sum,
):
    step = pl.program_id(0)

    @pl.when(step == 0)
    def _():
        sums_ref[...] = jnp.zeros_like(sums_ref)
        sums_ref[1:2, :] = gffn_ref[...]
        gw_sum[...] = jnp.zeros_like(gw_sum)

    dkv = kv0[...].astype(F32) + kv1[...].astype(F32) + kv2[...].astype(F32) + kv3[...].astype(F32)
    cos, sin = cos_ref[...], sin_ref[...]
    grads = []
    for h in range(3):
        grad = dq_ref[:, h * HD : (h + 1) * HD] if h < 2 else dkv[:, :HD]
        gain = qg_ref[...] if h < 2 else kg_ref[...]
        u = pre_ref[:, h * HD : (h + 1) * HD]
        rate = lax.rsqrt(jnp.mean(u * u, axis=-1, keepdims=True) + EPS)
        n = u * rate
        g = grad * cos - pltpu.roll(grad, HD // 2, 1) * sin
        gained = gain * g
        pre_grad = (gained - n * jnp.mean(gained * n, axis=-1, keepdims=True)) * rate
        grads.append(pre_grad.astype(BF))
        row = 2 if h < 2 else 3
        sums_ref[row : row + 1, :HD] += jnp.sum(g * n, axis=0, keepdims=True)
    gqkv = jnp.concatenate(grads + [dkv[:, HD:].astype(BF)], axis=1)
    gw_sum[...] += contract_first(norm_ref[...], gqkv)
    gnorm = contract_last(gqkv, w_ref[...])

    @pl.when(step < 2)
    def _():
        other_ref[...] = gnorm.astype(BF)

    @pl.when(step >= 2)
    def _():
        mine_ref[...] = gnorm.astype(BF)

    tok = tok_ref[...].astype(F32)
    xhat = tok * lax.rsqrt(jnp.mean(tok * tok, axis=-1, keepdims=True) + EPS)
    sums_ref[0:1, :] += jnp.sum(gnorm * xhat, axis=0, keepdims=True)

    @pl.when(step == 3)
    def _():
        gw_ref[:, : 4 * HD] = gw_sum[...].astype(BF)
        gw_ref[:, 4 * HD :] = gout_ref[...]


def project_back(dq, dkv, pre, cos, sin, q_gain, k_gain, tokens, w_qkv, norm, grad_out, grad_gain_ffn):
    rows, d = tokens.shape
    step = 256
    by_rows = lambda w: pl.BlockSpec((step, w), lambda i: ((i + 2) % 4, 0))
    whole = lambda a: pl.BlockSpec(a.shape, lambda i: (0, 0))
    return pl.pallas_call(
        qkv_back_kernel,
        grid=(rows // step,),
        in_specs=[by_rows(2 * HD)]
        + [by_rows(2 * HD)] * 4
        + [by_rows(3 * HD), by_rows(HD), by_rows(HD), whole(q_gain), whole(k_gain), by_rows(d), whole(w_qkv)]
        + [by_rows(d), whole(grad_out), whole(grad_gain_ffn)],
        out_specs=[
            pl.BlockSpec((d, 6 * HD), lambda i: (0, 0)),
            pl.BlockSpec((step, d), lambda i: (jnp.maximum(i - 2, 0), 0)),
            pl.BlockSpec((step, d), lambda i: (jnp.minimum(i, 1), 0)),
            pl.BlockSpec((16, d), lambda i: (0, 0)),
        ],
        out_shape=[
            jax.ShapeDtypeStruct((d, 6 * HD), BF),
            jax.ShapeDtypeStruct((rows // 2, d), BF),
            jax.ShapeDtypeStruct((rows // 2, d), BF),
            jax.ShapeDtypeStruct((16, d), F32),
        ],
        scratch_shapes=[pltpu.VMEM((d, 4 * HD), F32)],
        compiler_params=VMEM,
        cost_estimate=cost(1),
        name="project_back",
    )(dq, *dkv, pre, cos, sin, q_gain, k_gain, tokens, w_qkv, norm, grad_out, grad_gain_ffn)


def stacked(ref, i):
    rows = ref[pl.ds(pl.multiple_of(i * BLK, BLK), BLK), :]
    return jnp.concatenate([rows[:, :HD], rows[:, HD:]], axis=0)


def allowed_keys(start, place, first, count):
    pos = first + lax.broadcasted_iota(jnp.int32, (count, 2 * BLK), 0)
    return (pos >= start) & (pos <= place)


def query_places(qblk):
    lane = lax.broadcasted_iota(jnp.int32, (1, 2 * BLK), 1)
    return qblk * BLK + (lane & (BLK - 1))


def attend_kernel(kblk, qblk, low, start_ref, q_ref, kv0, kv1, kv2, kv3, out_ref, o_ref, lse_ref, keys, values_t):
    for s, ref in enumerate((kv0, kv1, kv2, kv3)):
        for j in range(8):
            at = pl.multiple_of(kblk[s * 8 + j] * BLK, BLK)
            keys[pl.ds(at, BLK), :] = ref[j * BLK : (j + 1) * BLK, :HD]
            values_t[:, pl.ds(at, BLK)] = ref[j * BLK : (j + 1) * BLK, HD:].T
    keys[KEYS:, :] = jnp.zeros((FWD_KEYS, HD), BF)
    values_t[:, KEYS:] = jnp.zeros((HD, FWD_KEYS), BF)

    def one_block(i, _):
        q = stacked(q_ref, i)
        start = start_ref[i]
        place = query_places(qblk[i])

        def one_chunk(c, carry):
            acc, total = carry
            first = pl.multiple_of((low[i] + c * (FWD_KEYS // BLK)) * BLK, BLK)
            scores = contract_last(keys[pl.ds(first, FWD_KEYS), :], q)
            ok = allowed_keys(start, place, first, FWD_KEYS)
            weights = jnp.where(ok, jnp.exp2(scores), 0.0)
            total = total + jnp.sum(weights.reshape(-1, 8, 2 * BLK), axis=0)
            acc = acc + dot(values_t[:, pl.ds(first, FWD_KEYS)], weights.astype(BF))
            return acc, total

        acc, total = lax.fori_loop(
            0,
            (qblk[i] - low[i]) // (FWD_KEYS // BLK) + 1,
            one_chunk,
            (jnp.zeros((HD, 2 * BLK), F32), jnp.zeros((8, 2 * BLK), F32)),
        )
        total = jnp.sum(total, axis=0, keepdims=True)
        o = acc * (1.0 / total)
        o_ref[i] = o
        lse_ref[i] = jnp.log2(total)
        rows = o.T.astype(BF)
        out_ref[pl.ds(pl.multiple_of(i * BLK, BLK), BLK), :] = jnp.concatenate([rows[:BLK], rows[BLK:]], axis=1)
        return 0

    lax.fori_loop(0, ROWS // BLK, one_block, 0)


def attend(kblk, qblk, low, start, q, kv):
    smem = pl.BlockSpec(memory_space=pltpu.SMEM)
    vmem = pl.BlockSpec(memory_space=pltpu.VMEM)
    blocks = ROWS // BLK
    return pl.pallas_call(
        attend_kernel,
        in_specs=[smem] * 3 + [vmem] * 6,
        out_specs=[vmem] * 3,
        out_shape=[
            jax.ShapeDtypeStruct((ROWS, 2 * HD), BF),
            jax.ShapeDtypeStruct((blocks, HD, 2 * BLK), F32),
            jax.ShapeDtypeStruct((blocks, 1, 2 * BLK), F32),
        ],
        scratch_shapes=[pltpu.VMEM((KEYS + FWD_KEYS, HD), BF), pltpu.VMEM((HD, KEYS + FWD_KEYS), BF)],
        compiler_params=VMEM,
        cost_estimate=cost(1),
        name="attend",
    )(kblk, qblk, low, start, q, *kv)


def attend_back_kernel(
    kblk, qblk, low, start_ref, q_ref, do_ref, o_ref, lse_ref, kv0, kv1, kv2, kv3,
    dq_ref, dkv0, dkv1, dkv2, dkv3, keys, keys_t, values, dk, dv,
):
    for s, ref in enumerate((kv0, kv1, kv2, kv3)):
        for j in range(8):
            at = pl.multiple_of(kblk[s * 8 + j] * BLK, BLK)
            key = ref[j * BLK : (j + 1) * BLK, :HD]
            keys[pl.ds(at, BLK), :] = key
            keys_t[:, pl.ds(at, BLK)] = key.T
            values[pl.ds(at, BLK), :] = ref[j * BLK : (j + 1) * BLK, HD:]
    dk[...] = jnp.zeros_like(dk)
    dv[...] = jnp.zeros_like(dv)
    keys[KEYS:, :] = jnp.zeros((BWD_KEYS, HD), BF)
    keys_t[:, KEYS:] = jnp.zeros((HD, BWD_KEYS), BF)
    values[KEYS:, :] = jnp.zeros((BWD_KEYS, HD), BF)

    def one_block(i, _):
        q = stacked(q_ref, i)
        do = stacked(do_ref, i)
        delta = jnp.sum(do.astype(F32).T * o_ref[i], axis=0, keepdims=True)
        lse = lse_ref[i]
        start = start_ref[i]
        place = query_places(qblk[i])

        def one_chunk(c, acc):
            first = pl.multiple_of((low[i] + c * (BWD_KEYS // BLK)) * BLK, BLK)
            here = pl.ds(first, BWD_KEYS)
            scores = contract_last(keys[here, :], q)
            ok = allowed_keys(start, place, first, BWD_KEYS)
            probs = jnp.where(ok, jnp.exp2(scores - lse), 0.0)
            dprobs = contract_last(values[here, :], do)
            dscores = (probs * (dprobs - delta)).astype(BF)
            dv[here, :] += dot(probs.astype(BF), do)
            dk[here, :] += dot(dscores, q)
            return acc + dot(keys_t[:, here], dscores)

        acc = lax.fori_loop(0, (qblk[i] - low[i]) // (BWD_KEYS // BLK) + 1, one_chunk, jnp.zeros((HD, 2 * BLK), F32))
        rows = acc.T * SCALE
        dq_ref[pl.ds(pl.multiple_of(i * BLK, BLK), BLK), :] = jnp.concatenate([rows[:BLK], rows[BLK:]], axis=1)
        return 0

    lax.fori_loop(0, ROWS // BLK, one_block, 0)
    for s, ref in enumerate((dkv0, dkv1, dkv2, dkv3)):
        for j in range(8):
            at = pl.multiple_of(kblk[s * 8 + j] * BLK, BLK)
            ref[j * BLK : (j + 1) * BLK, :HD] = (dk[pl.ds(at, BLK), :] * LN2).astype(BF)
            ref[j * BLK : (j + 1) * BLK, HD:] = dv[pl.ds(at, BLK), :].astype(BF)


def attend_back(kblk, qblk, low, start, q, do, o, lse, kv):
    smem = pl.BlockSpec(memory_space=pltpu.SMEM)
    vmem = pl.BlockSpec(memory_space=pltpu.VMEM)
    return pl.pallas_call(
        attend_back_kernel,
        in_specs=[smem] * 3 + [vmem] * 9,
        out_specs=[vmem] * 5,
        out_shape=[jax.ShapeDtypeStruct((ROWS, 2 * HD), F32)] + [jax.ShapeDtypeStruct((ROWS, 2 * HD), BF)] * 4,
        scratch_shapes=[
            pltpu.VMEM((KEYS + BWD_KEYS, HD), BF),
            pltpu.VMEM((HD, KEYS + BWD_KEYS), BF),
            pltpu.VMEM((KEYS + BWD_KEYS, HD), BF),
            pltpu.VMEM((KEYS + BWD_KEYS, HD), F32),
            pltpu.VMEM((KEYS + BWD_KEYS, HD), F32),
        ],
        compiler_params=VMEM,
        cost_estimate=cost(20),
        name="attend_back",
    )(kblk, qblk, low, start, q, do, o, lse, *kv)


def per_device(
    tokens,
    block_table,
    doc_ids,
    attn_gain,
    w_query,
    w_key,
    w_value,
    query_gain,
    key_gain,
    w_out,
    ffn_gain,
    w_gate,
    w_up,
    w_down,
    out_grad,
):
    ctx_rank = lax.axis_index("ctx")
    tp_rank = lax.axis_index("tp")
    x_lo, z, core = ctx_rank // 8, (ctx_rank // 2) % 4, ctx_rank % 2
    y, x_hi = tp_rank // 2, tp_rank % 2
    x = 2 * x_hi + x_lo
    d_model = tokens.shape[1]
    q_width, k_width, ff_local = w_query.shape[1], w_key.shape[1], w_gate.shape[1]

    ring = jnp.array(RING, jnp.int32)
    xs = ((x + ring) % 4)[None, None, :]
    zs = ((z + ring) % 4)[:, None, None]
    cores = ((core + jnp.arange(2, dtype=jnp.int32)) % 2)[None, :, None]
    entry = ((((xs % 2) * 4 + zs) * 2 + cores) * 2 + xs // 2).reshape(32)
    table = block_table.reshape(32)
    kblk = jnp.sum(
        jnp.where(entry[:, None] == jnp.arange(32, dtype=jnp.int32)[None, :], table[None, :], 0), axis=1
    ).astype(jnp.int32)
    qblk = kblk[:8]
    docs = lax.dynamic_index_in_dim(doc_ids, y, 0, keepdims=False)
    firsts = jnp.sum((docs[None, :] < jnp.arange(4, dtype=jnp.int32)[:, None]).astype(jnp.int32), axis=1)
    place = qblk[:, None] * BLK + jnp.arange(BLK, dtype=jnp.int32)[None, :]
    start = jnp.max(
        jnp.where(firsts[:, None, None] <= place[None], firsts[:, None, None], 0), axis=0
    )
    low = start[:, 0] // BLK
    start2 = jnp.concatenate([start, start], axis=1)[:, None, :]
    pos = (place - start).reshape(ROWS)
    freq = jnp.power(jnp.float32(THETA), -(jnp.arange(HD // 2, dtype=F32) * (2.0 / HD)))
    angles = pos.astype(F32)[:, None] * freq[None, :]
    cos_half, sin_half = jnp.cos(angles), jnp.sin(angles)
    cos = jnp.concatenate([cos_half, cos_half], axis=1)
    sin = jnp.concatenate([-sin_half, sin_half], axis=1)
    bits = ((y - jnp.arange(4, dtype=jnp.int32)) % 4)[None, :]
    offs = (((bits // 2) * 4 + zs.reshape(4, 1)) * 2 + bits % 2).reshape(16) * 64

    def head_gain(gain):
        return jnp.concatenate([gain, jnp.zeros((64 - gain.shape[0],), BF)])

    gains = jnp.stack([attn_gain, ffn_gain, head_gain(query_gain), head_gain(key_gain)], axis=1)
    gains = jnp.concatenate([gains, jnp.zeros((64, 124), BF)], axis=1)
    w_o, w_d = w_out.shape[0], w_down.shape[0]
    first_shard = jnp.concatenate([w_query, w_key, w_value, gains, w_out.T], axis=1)
    first_mine = jnp.concatenate(to_users(first_shard), axis=0)
    first = along_z(first_mine)
    w_qkv, gain_cols, w_proj = assembled(first, (q_width + 2 * k_width, 128, w_o), offs)
    gain_rows = gain_cols[:, :8].astype(F32).T
    gain_attn, gain_ffn = gain_rows[0:1], gain_rows[1:2]
    gain_query = gain_rows[2].reshape(16, 64)[:, :8].reshape(1, HD)
    gain_key = gain_rows[3].reshape(16, 64)[:, :8].reshape(1, HD)

    size = tokens.shape[0]
    rows_tok = gather_rows(after(tokens, first_shard))
    normal_one, q, kv, pre = project(rows_tok, gain_attn, w_qkv, gain_query, gain_key, cos, sin)
    kv_all = along_z(kv)
    own_grad, second = after((out_grad, jnp.concatenate([w_gate, w_up, w_down.T], axis=1)), kv)
    half_grad = jnp.concatenate([own_grad] + [shift(own_grad, dx=-d) for d in RING[1:]], axis=0)
    second = to_users(second)
    attn_low, o, lse = attend(kblk, qblk, low, start2, q, kv_all)
    attn_low, second, half_grad = lax.optimization_barrier((attn_low, second, half_grad))
    grad_rows = jnp.concatenate([half_grad, shift(half_grad, dcore=1)], axis=0)
    ffn_slots = along_z(jnp.concatenate(second, axis=0))
    both = sum_product(contract_last, attn_low, w_proj)
    resid = tokens.astype(F32) + summed(both, to_chips(both))
    rate_two = lax.rsqrt(jnp.mean(resid * resid, axis=-1, keepdims=True) + EPS)
    xhat_two = resid * rate_two
    rows_two = gather_rows(after((xhat_two * gain_ffn).astype(BF), ffn_slots[3]), gate=ffn_slots[1:3])
    w_gu, w_dn = assembled(ffn_slots, (2 * ff_local, w_d), offs)
    gate_up = dot(rows_two, w_gu)
    gate, up_proj = gate_up[:, :ff_local], gate_up[:, ff_local:]
    sigmoid_gate = jax.nn.sigmoid(gate)
    silu_gate = gate * sigmoid_gate
    hidden = (silu_gate * up_proj).astype(BF)
    grad_hidden = dot(grad_rows, w_dn)
    grad_gate = grad_hidden * up_proj * (sigmoid_gate * (1.0 + gate * (1.0 - sigmoid_gate)))
    grad_up = grad_hidden * silu_gate
    grad_gu = jnp.concatenate([grad_gate, grad_up], axis=1).astype(BF)
    both = sum_product(contract_last, grad_gu, w_gu)
    rows_now, grads_now, gu_now, hidden_now = after((rows_two, grad_rows, grad_gu, hidden), both)
    ffn_grads = jnp.concatenate([contract_first(rows_now, gu_now), contract_first(grads_now, hidden_now)], axis=1)
    ffn_parts = send_along_z(ffn_grads, z)
    half_rows = hidden.shape[0] // 2
    got_out = shift(contract_last(hidden_now[half_rows:], w_dn).astype(BF), dcore=1)
    grad_norm_two = summed(both, to_chips(both))
    grad_gain_ffn = jnp.sum(grad_norm_two * xhat_two, axis=0)
    gained = grad_norm_two * gain_ffn
    grad_resid = out_grad.astype(F32) + (
        gained - xhat_two * jnp.mean(gained * xhat_two, axis=-1, keepdims=True)
    ) * rate_two
    branch_rows = gather_rows(grad_resid.astype(BF), gate=ffn_parts[1:2])
    grad_attn = dot(branch_rows, w_proj).astype(BF)
    grad_attn = after(grad_attn, got_out)
    grad_out = contract_first(branch_rows, attn_low).astype(BF)

    dq, *dkv = attend_back(kblk, qblk, low, start2, q, grad_attn, o, lse, kv_all)
    dkv, ffn_parts[0], hidden = lax.optimization_barrier((dkv, ffn_parts[0], hidden))
    both_out = (contract_last(hidden[:half_rows], w_dn) + got_out.astype(F32)).astype(BF)
    ffn_low = sum_along_z(ffn_parts)
    dkv_all = [dkv[0]] + [shift(dkv[k], dz=RING[k]) for k in range(1, 4)]
    out = (resid + summed(both_out, to_chips(both_out))).astype(BF)
    ffn_owned = to_owners(after(ffn_low, dkv_all[1]), y)
    last_grads, mine, other, sums = project_back(
        dq, dkv_all, pre, cos, sin, gain_query, gain_key, rows_tok, w_qkv, normal_one, grad_out, grad_gain_ffn[None, :]
    )
    last_grads, mine, other, sums, out, ffn_owned = lax.optimization_barrier(
        (last_grads, mine, other, sums, out, ffn_owned)
    )
    last_parts = send_along_z(last_grads, z)
    other, sums = after((other, sums), last_grads)
    sums = (sums + shift(sums, dcore=1)).astype(BF)
    both = sum_cores(other, lambda got: mine.astype(F32) + got).reshape(4, size, d_model)
    both = jnp.concatenate([both, jnp.broadcast_to(sums[None], (4, 16, d_model))], axis=1).reshape(-1, d_model)
    one_parts = to_chips(both)
    grad_norm_one = summed(both, one_parts)
    grad_norm_one, sums = grad_norm_one[:size], grad_norm_one[size:]
    tok = tokens.astype(F32)
    rate_one = lax.rsqrt(jnp.mean(tok * tok, axis=-1, keepdims=True) + EPS)
    xhat_one = tok * rate_one
    gained = grad_norm_one * gain_attn
    grad_x = (
        grad_resid + (gained - xhat_one * jnp.mean(gained * xhat_one, axis=-1, keepdims=True)) * rate_one
    ).astype(BF)
    share, h_share = d_model // 16, HD // 16
    width = 2 * (share + h_share)
    shares = jnp.concatenate(
        [
            sums[0].reshape(16, share),
            sums[1].reshape(16, share),
            sums[2, :HD].reshape(16, h_share),
            sums[3, :HD].reshape(16, h_share),
            jnp.zeros((16, 256 - width), F32),
        ],
        axis=1,
    )
    shares = sum_along_z(send_along_z(shares.astype(BF), z))
    shares = jnp.pad(shares, ((0, 0), (0, 7), (0, last_grads.shape[1] - 256)))
    last_low = sum_along_z(after(last_parts, one_parts))
    last_owned = to_owners(jnp.concatenate([last_low, shares], axis=1), y)
    sums = last_owned[share]
    last_owned = last_owned[:share]
    w_all = q_width + 2 * k_width
    return (
        out,
        grad_x,
        sums[:share],
        last_owned[:, :q_width],
        last_owned[:, q_width : q_width + k_width],
        last_owned[:, q_width + k_width : w_all],
        sums[2 * share : 2 * share + h_share],
        sums[2 * share + h_share : width],
        last_owned[:, w_all:].T,
        sums[share : 2 * share],
        ffn_owned[:, :ff_local],
        ffn_owned[:, ff_local : 2 * ff_local],
        ffn_owned[:, 2 * ff_local :].T,
    )


def solution(mesh):
    in_specs = (
        P(("ctx", "tp"), None),
        P(),
        P(),
        P("ctx"),
        P("ctx", "tp"),
        P("ctx", "tp"),
        P("ctx", "tp"),
        P("ctx"),
        P("ctx"),
        P("tp", "ctx"),
        P("ctx"),
        P("ctx", "tp"),
        P("ctx", "tp"),
        P("tp", "ctx"),
        P(("ctx", "tp"), None),
    )
    out_specs = (
        P(("ctx", "tp"), None),
        P(("ctx", "tp"), None),
        P("ctx"),
        P("ctx", "tp"),
        P("ctx", "tp"),
        P("ctx", "tp"),
        P("ctx"),
        P("ctx"),
        P("tp", "ctx"),
        P("ctx"),
        P("ctx", "tp"),
        P("ctx", "tp"),
        P("tp", "ctx"),
    )
    return jax.shard_map(
        per_device, mesh=mesh, in_specs=in_specs, out_specs=out_specs, check_vma=False
    )
```
